32 devices in a mesh: groups: 2 (over y), expert: 4 (over z), role: 4 (over x, core).
Axes of the slice: x: 2, y: 2, z: 4, core: 2. Of those that a mesh axis runs over, the one named last changes fastest.
Arguments:
- tokens: bfloat16 [512, 7168], P(('groups', 'expert'), 'role'), parts along dimension 0, may hold values from -6 to 6
- routes: int32 [512, 8], P(('groups', 'expert')), parts along dimension 0, may hold values from 0 to 31, all different within a row; in each aligned block of 64 rows (0 to 63, 64 to 127, ...) at most 32 rows name the same one
- route_weights: float32 [512, 8], P(('groups', 'expert')), parts along dimension 0, may hold values from 0.1 to 1
- w_gate: bfloat16 [32, 7168, 1024], P('expert', 'role'), may hold values from -0.0625 to 0.0625
- w_up: bfloat16 [32, 7168, 1024], P('expert', 'role'), may hold values from -0.0625 to 0.0625
- w_down: bfloat16 [32, 1024, 7168], P('expert', None, 'role'), may hold values from -0.1875 to 0.1875
- latent: bfloat16 [512, 576], P(('groups', 'expert', 'role')), parts along dimension 0, may hold values from -400 to 400
- norm_gain: float32 [512], replicated, may hold values from 0.1 to 1.9
- prompt_lengths: int32 [16], P('groups'), parts along dimension 0, may hold values from 1 to 128, 256 in all
- span_offsets: int32 [16], P('groups'), parts along dimension 0, may hold values from 0 to 16383
- slot_source: int32 [32], P(('groups', 'expert', 'role')), parts along dimension 0, may hold values from 0 to 15, each once
Outputs:
- mixed_out: bfloat16 [512, 7168], P(('groups', 'expert'), 'role'), parts along dimension 0
- decode_cache: bfloat16 [32, 9216], P(('groups', 'expert', 'role')), parts along dimension 0
The draws below stay inside these ranges and needn't reach their ends.
There are 2 independent parts, one for each index of `groups`. The reference program is written for one: setup_inputs(seed, part) draws one part's arguments, and reference() takes and returns one part's arrays. A program takes and returns all parts, laid end to end along the dimension named above; an argument that names none is the same for every part. Nothing has to cross between parts.
Inputs may be any that keep to these rules, and one draw needn't show every extreme that they name: `routes`: within the 64 rows of one expert index no expert is named by more than 32 pairs, a bound that some block reaches; a row names 8 different experts. `slot_source`: each block number appears once.
All inputs are finite; a program needn't handle non-finite values.
Results may differ from the reference program's by a relative error of at most 0.0058.
Values may be sent and summed in bfloat16 or wider, within the bound.
A program may use at most 256 MiB of HBM per device.

```python
import math
import jax
import jax.numpy as jnp
import numpy as np
from jax import lax

D = 7168
FF = 1024
LAT = 512
ROPE = 64
EXPERTS = 32
TOP = 8
BLK = 16
NPROMPT = 8
TOK_E = 64
MOST = 32
TOKENS = 256
NBLK = 16
N_EXPERT = 4


def draw_latent(key, part):
    key = jax.random.fold_in(key, 11)
    key_col, key_row, key_base = jax.random.split(key, 3)
    col_scale = jnp.exp(jax.random.uniform(key_col, (LAT,), minval=0.0, maxval=math.log(10.0)))
    row_scale = jnp.exp(jax.random.uniform(key_row, (TOKENS, 1), minval=0.0, maxval=math.log(10.0)))
    base = jnp.clip(jax.random.normal(key_base, (TOKENS, LAT + ROPE)), -4.0, 4.0)
    scales = jnp.concatenate([row_scale * col_scale[None, :], jnp.ones((TOKENS, ROPE), jnp.float32)], axis=1)
    return (base * scales).astype(jnp.bfloat16)


def place_ends(values, rng, smallest, largest):
    longest = values.shape.index(max(values.shape))
    spots = []
    for shift in (0, 1):
        where = [jax.random.randint(jax.random.fold_in(rng, axis), (), 0, length) for axis, length in enumerate(values.shape)]
        where[longest] = (where[longest] + shift) % values.shape[longest]
        spots.append(tuple(where))
    return values.at[spots[0]].set(smallest).at[spots[1]].set(largest)


def levels(stream_key, extent, cuts, least, top_value):
    def one(axis_at, shards_of):
        steps = jax.random.uniform(jax.random.fold_in(jax.random.fold_in(stream_key, 6), axis_at), (shards_of,), jnp.float32, least / len(cuts), top_value / len(cuts))
        return jnp.repeat(jnp.exp(steps), extent[axis_at] // shards_of).reshape((-1,) + (1,) * (len(extent) - axis_at - 1))

    loudness = one(*cuts[0])
    for cut in cuts[1:]:
        loudness = loudness * one(*cut)
    return loudness


def profile(number_of, total, most, lean):
    weights = [(1 << 20) // math.isqrt(rank ** lean) + 1 for rank in range(2, number_of + 1)]
    rest, holding = total - most - (number_of - 1), [1] * (number_of - 1)
    while rest > 0:
        candidates = [i for i in range(number_of - 1) if holding[i] < most]
        mass, budget = sum([weights[i] for i in candidates]), rest
        for i in candidates:
            extra = min(most - holding[i], max(1, budget * weights[i] // mass), rest)
            holding[i] = holding[i] + extra
            rest = rest - extra
    return np.array([most] + holding)


def uneven_parts(stream_key, count, total, reach, skew):
    if count == 2:
        one = jax.random.randint(stream_key, (), max(1, total - reach), min(reach, total - 1) + 1)
        return jnp.stack([one, total - one])
    sizes = jnp.asarray(profile(count, total, reach, skew), jnp.int32)
    couples = (count - 1) // 2
    giver, taker = sizes[1:1 + 2 * couples:2], sizes[2:2 + 2 * couples:2]
    slack = jnp.minimum(giver - 1, reach - taker)
    shifted = jax.random.randint(jax.random.fold_in(stream_key, 1), (couples,), 0, 1 << 20) % (slack + 1)
    sizes = sizes.at[1:1 + 2 * couples:2].set(giver - shifted).at[2:2 + 2 * couples:2].set(taker + shifted)
    return sizes[jax.random.permutation(jax.random.fold_in(stream_key, 2), count)]


def assign_block(rng, own, number, rows, amount, top, reach, lean):
    sequence = jax.random.permutation(rng, amount)
    packed, usual = portions_of(amount, rows * top, reach, lean, True), portions_of(amount, rows * top, reach, lean, False)
    places = jnp.arange(amount)

    def named(sizes, turn):
        used = int((sizes > 0).sum())
        fixed = max(1, used // 4)
        moved = fixed + (places - fixed + turn * (used - fixed)) % max(1, amount - fixed)
        return jnp.zeros((amount,), jnp.int32).at[sequence[jnp.where(places < fixed, places, moved)]].set(jnp.asarray(sizes, jnp.int32))

    sizes = jnp.where(number % 4 == 0, named(packed, number // 4), named(usual, number - number // 4 - 1))
    mixed = jax.random.permutation(jax.random.fold_in(own, 3), amount)
    giver, taker = mixed[0:amount // 2 * 2:2], mixed[1:amount // 2 * 2:2]
    slack = jnp.minimum(sizes[giver] - 1, reach - sizes[taker]) // 2
    slack = jnp.where((giver == sequence[0]) | (taker == sequence[0]) | (sizes[taker] == 0), 0, jnp.maximum(slack, 0))
    moved = jax.random.randint(jax.random.fold_in(own, 4), (amount // 2,), 0, 1 << 20) % (slack + 1)
    sizes = sizes.at[giver].add(-moved).at[taker].add(moved)
    items = jnp.searchsorted(jnp.cumsum(sizes), jnp.arange(rows * top), side="right").astype(jnp.int32)
    grid = items.reshape(top, rows).T
    grid = grid[jax.random.permutation(jax.random.fold_in(own, 1), rows)]
    turn = jax.random.randint(jax.random.fold_in(own, 2), (rows, 1), 0, top)
    return jnp.take_along_axis(grid, (jnp.arange(top)[None, :] + turn) % top, axis=1)


def portions_of(amount, total, bound, lean, full):
    portions = [(1 << 20) // math.isqrt(grade ** lean) + 1 for grade in range(1, amount + 1)]
    largest = bound if full else min(bound, max(-(-total // amount), total * portions[0] // sum(portions)))
    least = 1 if total - largest >= amount - 1 else 0
    holding, rest = [largest] + [least] * (amount - 1), total - largest - least * (amount - 1)
    while rest > 0:
        candidates = [i for i in range(1, amount) if holding[i] < largest] or [i for i in range(1, amount) if holding[i] < bound]
        mass, remaining = sum([portions[i] for i in candidates]), rest
        for i in candidates:
            extra = min(bound - holding[i], max(1, remaining * portions[i] // mass), rest)
            holding[i] = holding[i] + extra
            rest = rest - extra
    return np.array(holding)


def centred(stream_key, shape, deviation, most, cuts=(), held_as=jnp.bfloat16):
    level = levels(stream_key, shape, cuts, -0.22, 0.18) if cuts else 1.0
    array = jax.random.normal(stream_key, shape, jnp.float32) * deviation * level
    return jnp.minimum(jnp.maximum(array, -most), most).astype(held_as)


def setup_inputs(seed: int = 0, part: int = 0) -> dict:
    streams_of = jax.random.split(jax.random.key(seed), 12)
    own_keys = jax.random.split(jax.random.fold_in(streams_of[11], part), 12)
    tokens = centred(own_keys[0], (TOKENS, D), 1.0, 6.0, ((0, 4), (1, 4)))
    routes_keys = jax.random.split(jax.random.fold_in(own_keys[1], 1), TOKENS // TOK_E)
    routes_turns = jax.random.permutation(jax.random.fold_in(own_keys[1], 3), TOKENS // TOK_E)
    routes = jax.vmap(lambda own, number: assign_block(jax.random.fold_in(own_keys[1], 2), own, number, TOK_E, EXPERTS, TOP, MOST, 2))(routes_keys, routes_turns).reshape((TOKENS, TOP))
    route_weights = jnp.clip(0.1 + 0.9 * jax.random.uniform(own_keys[2], (TOKENS, TOP), jnp.float32) ** levels(own_keys[2], (TOKENS, TOP), ((0, 4),), -0.2, 0.2), 0.1, 1.0)
    w_gate = centred(streams_of[3], (EXPERTS, D, FF), D ** -0.5, 0.0625, ((0, 4), (1, 4)))
    w_up = centred(streams_of[4], (EXPERTS, D, FF), D ** -0.5, 0.0625, ((0, 4), (1, 4)))
    w_down = centred(streams_of[5], (EXPERTS, FF, D), FF ** -0.5, 0.1875, ((0, 4), (2, 4)))
    latent = draw_latent(jax.random.fold_in(jax.random.fold_in(streams_of[11], part), 71), part)
    norm_gain = jnp.clip(1.0 + 0.18 * jax.random.normal(streams_of[7], (LAT,), jnp.float32), 0.1, 1.9)
    prompt_lengths = uneven_parts(own_keys[8], NPROMPT, TOKENS, TOKENS // 2, 2).astype(jnp.int32)
    span_offsets = place_ends(jax.random.randint(own_keys[9], (NPROMPT,), 0, 16384), jax.random.fold_in(own_keys[9], 1), 0, 16383).astype(jnp.int32)
    slot_source = jax.random.permutation(own_keys[10], NBLK).astype(jnp.int32)
    return {"tokens": tokens, "routes": routes, "route_weights": route_weights, "w_gate": w_gate, "w_up": w_up, "w_down": w_down, "latent": latent, "norm_gain": norm_gain, "prompt_lengths": prompt_lengths, "span_offsets": span_offsets, "slot_source": slot_source}


def token_positions(token_index, prompt_lengths, span_offsets):
    starts = jnp.cumsum(prompt_lengths) - prompt_lengths
    inside = (token_index[:, None] >= starts[None, :]) & (token_index[:, None] < (starts + prompt_lengths)[None, :])
    placed = span_offsets[None, :] + token_index[:, None] - starts[None, :]
    return lax.optimization_barrier(jnp.sum(jnp.where(inside, placed, 0), axis=1)).astype(jnp.float32)

def latent_rows(latent, norm_gain, positions_f):
    latent_f = latent.astype(jnp.float32)
    compressed = latent_f[:, :LAT]
    rope_part = latent_f[:, LAT:]
    normed = compressed * lax.rsqrt(lax.optimization_barrier(jnp.mean(compressed * compressed, axis=1, keepdims=True)) + 1e-06) * norm_gain[None, :]
    half_rope = ROPE // 2
    inverse_freq = jnp.exp(jnp.arange(half_rope, dtype=jnp.float32) * (-2.0 * math.log(10000.0) / ROPE))
    angles = positions_f[:, None] * inverse_freq[None, :]
    cosine = jnp.cos(angles)
    sine_part = jnp.sin(angles)
    first_half = rope_part[:, :half_rope]
    second_half = rope_part[:, half_rope:]
    rotated = jnp.concatenate([first_half * cosine - second_half * sine_part, second_half * cosine + first_half * sine_part], axis=1)
    return jnp.concatenate([normed, rotated], axis=1).astype(jnp.bfloat16)

def reference(tokens, routes, route_weights, w_gate, w_up, w_down, latent, norm_gain, prompt_lengths, span_offsets, slot_source):
    capacity = N_EXPERT * MOST
    flat_routes = routes.reshape(-1)
    pair_tok = jnp.arange(TOKENS * TOP, dtype=jnp.int32) // TOP

    def through_expert(running, stacked):
        expert_id, gate_w, up_w, down_w = stacked
        routed = (flat_routes == expert_id).astype(jnp.int32)
        ranking = jnp.cumsum(routed) - 1
        slot_index = jnp.where(routed > 0, ranking, capacity).astype(jnp.int32)
        slot_table = jnp.zeros((capacity + 1,), jnp.int32).at[slot_index].set(pair_tok)[:capacity]
        chosen = tokens[slot_table]
        gate_act = jnp.dot(chosen, gate_w, preferred_element_type=jnp.float32)
        up_act = jnp.dot(chosen, up_w, preferred_element_type=jnp.float32)
        hidden = (jax.nn.silu(gate_act) * up_act).astype(jnp.bfloat16)
        expert_out = jnp.dot(hidden, down_w, preferred_element_type=jnp.float32).astype(jnp.bfloat16)
        padded = jnp.concatenate([expert_out, jnp.zeros((1, D), jnp.bfloat16)], axis=0)
        slot_pairs = slot_index.reshape(TOKENS, TOP)
        for route_slot in range(TOP):
            picked = padded[slot_pairs[:, route_slot]]
            running = running + route_weights[:, route_slot:route_slot + 1] * picked.astype(jnp.float32)
        return (running, None)
    running = jnp.zeros((TOKENS, D), jnp.float32)
    stacked = (jnp.arange(EXPERTS, dtype=jnp.int32), w_gate, w_up, w_down)
    running, unused = lax.scan(through_expert, running, stacked)
    mixed_out = running.astype(jnp.bfloat16)
    token_index = jnp.arange(TOKENS, dtype=jnp.int32)
    positions_f = token_positions(token_index, prompt_lengths, span_offsets)
    cache_rows = latent_rows(latent, norm_gain, positions_f)
    blocks = cache_rows.reshape(NBLK, BLK * (LAT + ROPE))
    decode_cache = blocks[slot_source]
    return (mixed_out, decode_cache)
```

```python
import functools
import math

import jax
import jax.numpy as jnp
from jax import lax
from jax.experimental import pallas as pl
from jax.experimental.pallas import tpu as pltpu
from jax.sharding import PartitionSpec as P

LAT = 512
ROPE = 64
EXPERTS = 32
BLK = 16
MOST = 32


def token_positions(token_index, prompt_lengths, span_offsets):
    starts = jnp.cumsum(prompt_lengths) - prompt_lengths
    inside = (token_index[:, None] >= starts[None, :]) & (
        token_index[:, None] < (starts + prompt_lengths)[None, :]
    )
    placed = span_offsets[None, :] + token_index[:, None] - starts[None, :]
    return jnp.sum(jnp.where(inside, placed, 0), axis=1).astype(jnp.float32)


def latent_rows(latent, norm_gain, positions_f):
    latent_f = latent.astype(jnp.float32)
    compressed = latent_f[:, :LAT]
    rope_part = latent_f[:, LAT:]
    normed = (
        compressed
        * lax.rsqrt(jnp.mean(compressed * compressed, axis=1, keepdims=True) + 1e-06)
        * norm_gain[None, :]
    )
    half_rope = ROPE // 2
    inverse_freq = jnp.exp(
        jnp.arange(half_rope, dtype=jnp.float32) * (-2.0 * math.log(10000.0) / ROPE)
    )
    angles = positions_f[:, None] * inverse_freq[None, :]
    cosine = jnp.cos(angles)
    sine_part = jnp.sin(angles)
    first_half = rope_part[:, :half_rope]
    second_half = rope_part[:, half_rope:]
    rotated = jnp.concatenate(
        [
            first_half * cosine - second_half * sine_part,
            second_half * cosine + first_half * sine_part,
        ],
        axis=1,
    )
    return jnp.concatenate([normed, rotated], axis=1).astype(jnp.bfloat16)


GATE_SLOTS = 4
DOWN_SLOTS = 5
VMEM_LIMIT = 62 * 1024 * 1024


def fits_kernel(tokens, w_gate):
    return (
        lax.axis_size("role") == 4
        and lax.axis_size("expert") * MOST <= 128
        and w_gate.shape[0] >= DOWN_SLOTS
    )


def moe_kernel(
    sources,
    tok_ref,
    routes_ref,
    rw_ref,
    wg_ref,
    wu_ref,
    wd_ref,
    out_ref,
    tok_all,
    info_all,
    info_mine,
    info_row,
    wslots,
    dslots,
    xbuf,
    own,
    send1,
    recv1,
    send2,
    recv2,
    hid,
    hs,
    acc,
    psend,
    precv,
    wsem,
    dsem,
    tok_send,
    tok_recv,
    info_send,
    info_recv,
    s1_send,
    s1_recv,
    s2_send,
    s2_recv,
    h_send,
    h_recv,
    p_send,
    p_recv,
):
    z = lax.axis_index("expert")
    role = lax.axis_index("role")
    chip = lax.div(role, 2)
    core = lax.rem(role, 2)
    core_peer = {"role": chip * 2 + (1 - core)}
    chip_peer = {"role": (1 - chip) * 2 + core}
    experts = wg_ref.shape[0]
    count = tok_ref.shape[0]
    width = tok_ref.shape[1]
    ff = wg_ref.shape[2]
    half = ff // 2
    quarter = ff // 4
    slots = sources * MOST
    peers = [{"expert": lax.rem(z + d, sources)} for d in range(1, sources)]

    def weight_copy(ref, which, e):
        slot = lax.rem(2 * e + which, GATE_SLOTS)
        return pltpu.make_async_copy(ref.at[e], wslots.at[slot], wsem.at[slot])

    def down_copy(e):
        slot = lax.rem(e, DOWN_SLOTS)
        return pltpu.make_async_copy(wd_ref.at[e], dslots.at[slot], dsem.at[slot])

    for e in range(GATE_SLOTS // 2):
        weight_copy(wg_ref, 0, e).start()
        weight_copy(wu_ref, 1, e).start()
    for e in range(DOWN_SLOTS):
        down_copy(e).start()

    barrier = pltpu.get_barrier_semaphore()
    everyone = peers + [core_peer, chip_peer]
    for peer in everyone:
        pl.semaphore_signal(barrier, inc=1, device_id=peer, device_id_type=pl.DeviceIdType.MESH)
    pl.semaphore_wait(barrier, len(everyone))

    def remote(src, dst, send_sem, recv_sem, peer):
        return pltpu.make_async_remote_copy(
            src_ref=src,
            dst_ref=dst,
            send_sem=send_sem,
            recv_sem=recv_sem,
            device_id=peer,
            device_id_type=pl.DeviceIdType.MESH,
        )

    def token_copy(d):
        return remote(
            tok_ref, tok_all.at[pl.ds(d * count, count)], tok_send.at[d], tok_recv.at[d], peers[d - 1]
        )

    def info_copy(d):
        return remote(info_mine, info_all.at[d], info_send.at[d], info_recv.at[d], peers[d - 1])

    expert_id = lax.broadcasted_iota(jnp.int32, (EXPERTS, count), 0)
    member = jnp.zeros((EXPERTS, count), jnp.float32)
    weight = jnp.zeros((EXPERTS, count), jnp.float32)
    for k in range(routes_ref.shape[0]):
        hit = routes_ref[k : k + 1, :] == expert_id
        member = member + jnp.where(hit, 1.0, 0.0)
        weight = weight + jnp.where(hit, rw_ref[k : k + 1, :], 0.0)
    before = jnp.where(
        lax.broadcasted_iota(jnp.int32, (count, count), 0)
        < lax.broadcasted_iota(jnp.int32, (count, count), 1),
        1.0,
        0.0,
    ).astype(jnp.bfloat16)
    rank = jnp.dot(member.astype(jnp.bfloat16), before, preferred_element_type=jnp.float32)
    info_mine[0:EXPERTS, 0:count] = jnp.where(member > 0.5, rank, -1000.0)
    info_mine[EXPERTS : 2 * EXPERTS, 0:count] = weight
    info_mine[:, count:] = jnp.zeros((2 * EXPERTS, info_mine.shape[1] - count), jnp.float32)

    for d in range(1, sources):
        info_copy(d).start()
    for d in range(1, sources):
        token_copy(d).start()
    tok_all[0:count, :] = tok_ref[...]
    for d in range(1, sources):
        info_copy(d).wait_recv()
    rows = [info_mine[:, 0:count]] + [info_all[d, :, 0:count] for d in range(1, sources)]
    rows = [r + jnp.where(
        lax.broadcasted_iota(jnp.int32, r.shape, 0) < EXPERTS, float(d * MOST), 0.0
    ) for d, r in enumerate(rows)]
    info_row[...] = jnp.concatenate(rows, axis=1)
    for d in range(1, sources):
        token_copy(d).wait_recv()

    slot_id = lax.broadcasted_iota(jnp.int32, (slots, sources * count), 0).astype(jnp.float32)

    def placing(e):
        row = info_row[pl.ds(z * experts + e, 1), :]
        return row == slot_id

    def core_copy(e):
        return remote(send1.at[e], recv1.at[e], s1_send.at[e], s1_recv.at[e], core_peer)

    def chip_copy(e):
        return remote(send2.at[e], recv2.at[e], s2_send.at[e], s2_recv.at[e], chip_peer)

    mine = core * 2 + chip
    theirs = core * 2 + (1 - chip)

    def hid_copy(e, kind):
        q = mine if kind < 2 else theirs
        peer = chip_peer if kind == 0 else core_peer
        return remote(hid.at[e, q], hid.at[e, q], h_send.at[e, kind], h_recv.at[e, kind], peer)

    def project(e):
        weight_copy(wg_ref, 0, e).wait()
        weight_copy(wu_ref, 1, e).wait()
        one_hot = jnp.where(placing(e), 1.0, 0.0).astype(jnp.bfloat16)
        xbuf[...] = jnp.dot(
            one_hot, tok_all[...], preferred_element_type=jnp.float32
        ).astype(jnp.bfloat16)
        gate_slot = lax.rem(2 * e, GATE_SLOTS)
        for where_to, part in ((send1, 1 - core), (own, core)):
            cols = pl.ds(pl.multiple_of(part * half, half), half)
            for which in range(2):
                where_to[e, :, which * half : (which + 1) * half] = jnp.dot(
                    xbuf[...],
                    wslots[gate_slot + which, :, cols],
                    preferred_element_type=jnp.float32,
                )
            if where_to is send1:
                core_copy(e).start()

        @pl.when(e + GATE_SLOTS // 2 < experts)
        def _():
            weight_copy(wg_ref, 0, e + GATE_SLOTS // 2).start()
            weight_copy(wu_ref, 1, e + GATE_SLOTS // 2).start()

    def add_core(e):
        core_copy(e).wait_recv()
        for which in range(2):
            keep = pl.ds(pl.multiple_of(which * half + chip * quarter, quarter), quarter)
            give = pl.ds(pl.multiple_of(which * half + (1 - chip) * quarter, quarter), quarter)
            send2[e, :, which * quarter : (which + 1) * quarter] = (
                own[e, :, give] + recv1[e, :, give]
            ).astype(jnp.bfloat16)
        chip_copy(e).start()
        for which in range(2):
            keep = pl.ds(pl.multiple_of(which * half + chip * quarter, quarter), quarter)
            own[e, :, keep] = own[e, :, keep] + recv1[e, :, keep]

    def activate(e):
        chip_copy(e).wait_recv()
        sums = []
        for which in range(2):
            keep = pl.ds(pl.multiple_of(which * half + chip * quarter, quarter), quarter)
            got = recv2[e, :, which * quarter : (which + 1) * quarter]
            sums.append(own[e, :, keep] + got.astype(jnp.float32))
        w_row = info_row[pl.ds(EXPERTS + z * experts + e, 1), :]
        w_slot = jnp.sum(jnp.where(placing(e), w_row, 0.0), axis=1, keepdims=True)
        hid[e, mine] = (jax.nn.silu(sums[0]) * sums[1] * w_slot).astype(jnp.bfloat16)
        hid_copy(e, 0).start()
        hid_copy(e, 1).start()

    def forward(e):
        hid_copy(e, 0).wait_recv()
        hid_copy(e, 2).start()

    def finish(e):
        hid_copy(e, 1).wait_recv()
        hid_copy(e, 2).wait_recv()
        one_hot = jnp.where(placing(e), 1.0, 0.0).astype(jnp.bfloat16)
        for q in range(4):
            hs[:, q * quarter : (q + 1) * quarter] = lax.dot_general(
                one_hot,
                hid[e, q],
                (((0,), (0,)), ((), ())),
                preferred_element_type=jnp.float32,
            ).astype(jnp.bfloat16)
        down_copy(e).wait()
        slot = lax.rem(e, DOWN_SLOTS)

        def columns(j, carry):
            cols = pl.ds(pl.multiple_of(j * 256, 256), 256)
            acc[:, cols] += jnp.dot(
                hs[...], dslots[slot, :, cols], preferred_element_type=jnp.float32
            )
            return carry

        lax.fori_loop(0, width // 256, columns, 0)

        @pl.when(e + DOWN_SLOTS < experts)
        def _():
            down_copy(e + DOWN_SLOTS).start()

    acc[...] = jnp.zeros_like(acc)

    def step(i, carry):
        for lag, stage in enumerate((project, add_core, activate, forward, finish)):

            @pl.when((i >= lag) & (i - lag < experts))
            def _():
                stage(i - lag)

        return carry

    lax.fori_loop(0, experts + 4, step, 0)

    def back_copy(d):
        return remote(
            psend.at[d], precv.at[d], p_send.at[d], p_recv.at[d], {"expert": lax.rem(z + sources - d, sources)}
        )

    for d in range(1, sources):
        psend[d] = acc[d * count : (d + 1) * count, :].astype(jnp.bfloat16)
        back_copy(d).start()
    total = acc[0:count, :]
    for d in range(1, sources):
        back_copy(d).wait_recv()
        total = total + precv[d].astype(jnp.float32)
    out_ref[...] = total.astype(out_ref.dtype)

    for d in range(1, sources):
        info_copy(d).wait_send()
        token_copy(d).wait_send()
        back_copy(d).wait_send()

    def drain(e, carry):
        core_copy(e).wait_send()
        chip_copy(e).wait_send()
        for kind in range(3):
            hid_copy(e, kind).wait_send()
        return carry

    lax.fori_loop(0, experts, drain, 0)


def experts_kernel(tokens, routes, route_weights, w_gate, w_up, w_down):
    sources = lax.axis_size("expert")
    count, width = tokens.shape
    experts, _, ff = w_gate.shape
    slots = sources * MOST
    half, quarter = ff // 2, ff // 4
    bf16, f32 = jnp.bfloat16, jnp.float32
    vmem = pl.BlockSpec(memory_space=pltpu.VMEM)
    hbm = pl.BlockSpec(memory_space=pl.ANY)
    dma = pltpu.SemaphoreType.DMA
    return pl.pallas_call(
        functools.partial(moe_kernel, sources),
        out_shape=jax.ShapeDtypeStruct((count, width), bf16),
        in_specs=[vmem, vmem, vmem, hbm, hbm, hbm],
        out_specs=vmem,
        scratch_shapes=[
            pltpu.VMEM((sources * count, width), bf16),
            pltpu.VMEM((sources, 2 * EXPERTS, 128), f32),
            pltpu.VMEM((2 * EXPERTS, 128), f32),
            pltpu.VMEM((2 * EXPERTS, sources * count), f32),
            pltpu.VMEM((GATE_SLOTS, width, ff), bf16),
            pltpu.VMEM((DOWN_SLOTS, ff, width), bf16),
            pltpu.VMEM((slots, width), bf16),
            pltpu.VMEM((experts, slots, ff), f32),
            pltpu.VMEM((experts, slots, ff), f32),
            pltpu.VMEM((experts, slots, ff), f32),
            pltpu.VMEM((experts, slots, half), bf16),
            pltpu.VMEM((experts, slots, half), bf16),
            pltpu.VMEM((experts, 4, slots, quarter), bf16),
            pltpu.VMEM((sources * count, ff), bf16),
            pltpu.VMEM((sources * count, width), f32),
            pltpu.VMEM((sources, count, width), bf16),
            pltpu.VMEM((sources, count, width), bf16),
            dma((GATE_SLOTS,)),
            dma((DOWN_SLOTS,)),
            dma((sources,)),
            dma((sources,)),
            dma((sources,)),
            dma((sources,)),
            dma((experts,)),
            dma((experts,)),
            dma((experts,)),
            dma((experts,)),
            dma((experts, 3)),
            dma((experts, 3)),
            dma((sources,)),
            dma((sources,)),
        ],
        compiler_params=pltpu.CompilerParams(
            collective_id=0, has_side_effects=True, vmem_limit_bytes=VMEM_LIMIT
        ),
        cost_estimate=pl.CostEstimate(
            flops=8 * experts * slots * width * ff,
            bytes_accessed=6 * experts * width * ff,
            transcendentals=0,
        ),
    )(tokens, routes.T, route_weights.T, w_gate, w_up, w_down)


def experts_plain(tokens, routes, route_weights, w_gate, w_up, w_down):
    experts_here = w_gate.shape[0]
    token_count = routes.shape[0]
    route_count = routes.shape[1]
    feat_width = tokens.shape[1]
    expert_devices = lax.axis_size("expert")
    flat_routes = routes.reshape(-1)
    onehot = (flat_routes[:, None] == jnp.arange(EXPERTS, dtype=jnp.int32)[None, :]).astype(
        jnp.int32
    )
    earlier = jnp.cumsum(onehot, axis=0) - onehot
    dest_row = flat_routes * MOST + jnp.sum(earlier * onehot, axis=1)
    pair_tok = jnp.arange(token_count * route_count, dtype=jnp.int32) // route_count
    slot_table = jnp.full((EXPERTS * MOST,), token_count, jnp.int32).at[dest_row].set(pair_tok)
    padded = jnp.concatenate([tokens, jnp.zeros((1, feat_width), tokens.dtype)], axis=0)
    outgoing = padded[slot_table]
    incoming = lax.all_to_all(outgoing, "expert", split_axis=0, concat_axis=0, tiled=True)
    grouped = incoming.reshape(expert_devices, experts_here, MOST, feat_width)
    gate_part = jnp.einsum("secd,edf->secf", grouped, w_gate, preferred_element_type=jnp.float32)
    up_part = jnp.einsum("secd,edf->secf", grouped, w_up, preferred_element_type=jnp.float32)
    gate_act, up_act = lax.psum((gate_part, up_part), "role")
    hidden = (jax.nn.silu(gate_act) * up_act).astype(jnp.bfloat16)
    result = jnp.einsum(
        "secf,efd->secd", hidden, w_down, preferred_element_type=jnp.float32
    ).astype(jnp.bfloat16)
    returned = lax.all_to_all(
        result.reshape(expert_devices * experts_here * MOST, feat_width),
        "expert",
        split_axis=0,
        concat_axis=0,
        tiled=True,
    )
    picked = returned[dest_row].reshape(token_count, route_count, feat_width)
    mixed_out = jnp.sum(picked * route_weights[:, :, None], axis=1).astype(jnp.bfloat16)
    return mixed_out


def decode_blocks(latent, norm_gain, prompt_lengths, span_offsets, slot_source):
    latent_count = latent.shape[0]
    token_index = lax.axis_index(("expert", "role")) * latent_count + jnp.arange(
        latent_count, dtype=jnp.int32
    )
    positions_f = token_positions(token_index, prompt_lengths, span_offsets)
    cache_rows = latent_rows(latent, norm_gain, positions_f)
    blocks = cache_rows.reshape(latent_count // BLK, BLK * latent.shape[1])
    shard_piece = lax.all_gather(blocks, ("expert", "role"), axis=0, tiled=True)
    block_ids = jnp.arange(shard_piece.shape[0], dtype=jnp.int32)
    picker = (slot_source[:, None] == block_ids[None, :]).astype(jnp.bfloat16)
    decode_cache = jnp.dot(picker, shard_piece, preferred_element_type=jnp.float32).astype(
        jnp.bfloat16
    )
    return decode_cache


def local(
    tokens,
    routes,
    route_weights,
    w_gate,
    w_up,
    w_down,
    latent,
    norm_gain,
    prompt_lengths,
    span_offsets,
    slot_source,
):
    decode_cache = decode_blocks(latent, norm_gain, prompt_lengths, span_offsets, slot_source)
    if fits_kernel(tokens, w_gate):
        mixed_out = experts_kernel(tokens, routes, route_weights, w_gate, w_up, w_down)
    else:
        mixed_out = experts_plain(tokens, routes, route_weights, w_gate, w_up, w_down)
    return (mixed_out, decode_cache)


def solution(mesh):
    in_specs = (
        P(("groups", "expert"), "role"),
        P(("groups", "expert"), None),
        P(("groups", "expert"), None),
        P("expert", "role", None),
        P("expert", "role", None),
        P("expert", None, "role"),
        P(("groups", "expert", "role"), None),
        P(),
        P("groups"),
        P("groups"),
        P(("groups", "expert", "role")),
    )
    out_specs = (P(("groups", "expert"), "role"), P(("groups", "expert", "role"), None))
    return jax.shard_map(local, mesh=mesh, in_specs=in_specs, out_specs=out_specs, check_vma=False)
```

```python
import functools
import math

import jax
import jax.numpy as jnp
from jax import lax
from jax.experimental import pallas as pl
from jax.experimental.pallas import tpu as pltpu
from jax.sharding import PartitionSpec as P

LAT = 512
ROPE = 64
EXPERTS = 32
BLK = 16
MOST = 32


def token_positions(token_index, prompt_lengths, span_offsets):
    starts = jnp.cumsum(prompt_lengths) - prompt_lengths
    inside = (token_index[:, None] >= starts[None, :]) & (
        token_index[:, None] < (starts + prompt_lengths)[None, :]
    )
    placed = span_offsets[None, :] + token_index[:, None] - starts[None, :]
    return jnp.sum(jnp.where(inside, placed, 0), axis=1).astype(jnp.float32)


def latent_rows(latent, norm_gain, positions_f):
    latent_f = latent.astype(jnp.float32)
    compressed = latent_f[:, :LAT]
    rope_part = latent_f[:, LAT:]
    normed = (
        compressed
        * lax.rsqrt(jnp.mean(compressed * compressed, axis=1, keepdims=True) + 1e-06)
        * norm_gain[None, :]
    )
    half_rope = ROPE // 2
    inverse_freq = jnp.exp(
        jnp.arange(half_rope, dtype=jnp.float32) * (-2.0 * math.log(10000.0) / ROPE)
    )
    angles = positions_f[:, None] * inverse_freq[None, :]
    cosine = jnp.cos(angles)
    sine_part = jnp.sin(angles)
    first_half = rope_part[:, :half_rope]
    second_half = rope_part[:, half_rope:]
    rotated = jnp.concatenate(
        [
            first_half * cosine - second_half * sine_part,
            second_half * cosine + first_half * sine_part,
        ],
        axis=1,
    )
    return jnp.concatenate([normed, rotated], axis=1).astype(jnp.bfloat16)


GATE_SLOTS = 4
DOWN_SLOTS = 5
VMEM_LIMIT = 62 * 1024 * 1024


def fits_kernel(w_gate, latent):
    return (
        lax.axis_size("role") == 4
        and lax.axis_size("expert") * MOST <= 128
        and w_gate.shape[0] >= DOWN_SLOTS
        and latent.shape[0] == BLK
    )


def moe_kernel(
    sources,
    tok_ref,
    routes_ref,
    rw_ref,
    wg_ref,
    wu_ref,
    wd_ref,
    rows_ref,
    source_ref,
    out_ref,
    decode_ref,
    tok_all,
    info_all,
    info_mine,
    info_row,
    wslots,
    dslots,
    xbuf,
    own,
    send1,
    recv1,
    send2,
    recv2,
    hid,
    hs,
    acc,
    psend,
    precv,
    wsem,
    dsem,
    tok_send,
    tok_recv,
    info_send,
    info_recv,
    s1_send,
    s1_recv,
    s2_send,
    s2_recv,
    h_send,
    h_recv,
    p_send,
    p_recv,
    cache_all,
    c_send,
    c_recv,
):
    z = lax.axis_index("expert")
    role = lax.axis_index("role")
    chip = lax.div(role, 2)
    core = lax.rem(role, 2)
    core_peer = {"role": chip * 2 + (1 - core)}
    chip_peer = {"role": (1 - chip) * 2 + core}
    experts = wg_ref.shape[0]
    count = tok_ref.shape[0]
    width = tok_ref.shape[1]
    ff = wg_ref.shape[2]
    half = ff // 2
    quarter = ff // 4
    slots = sources * MOST
    peers = [{"expert": lax.rem(z + d, sources)} for d in range(1, sources)]

    def weight_copy(ref, which, e):
        slot = lax.rem(2 * e + which, GATE_SLOTS)
        return pltpu.make_async_copy(ref.at[e], wslots.at[slot], wsem.at[slot])

    def down_copy(e):
        slot = lax.rem(e, DOWN_SLOTS)
        return pltpu.make_async_copy(wd_ref.at[e], dslots.at[slot], dsem.at[slot])

    for e in range(GATE_SLOTS // 2):
        weight_copy(wg_ref, 0, e).start()
        weight_copy(wu_ref, 1, e).start()
    for e in range(DOWN_SLOTS):
        down_copy(e).start()

    barrier = pltpu.get_barrier_semaphore()
    everyone = peers + [core_peer, chip_peer]
    for peer in everyone:
        pl.semaphore_signal(barrier, inc=1, device_id=peer, device_id_type=pl.DeviceIdType.MESH)
    pl.semaphore_wait(barrier, len(everyone))

    def remote(src, dst, send_sem, recv_sem, peer):
        return pltpu.make_async_remote_copy(
            src_ref=src,
            dst_ref=dst,
            send_sem=send_sem,
            recv_sem=recv_sem,
            device_id=peer,
            device_id_type=pl.DeviceIdType.MESH,
        )

    def token_copy(d):
        return remote(
            tok_ref, tok_all.at[pl.ds(d * count, count)], tok_send.at[d], tok_recv.at[d], peers[d - 1]
        )

    def info_copy(d):
        return remote(info_mine, info_all.at[d], info_send.at[d], info_recv.at[d], peers[d - 1])

    def block_copy(kind):
        place = cache_all.at[z, chip if kind < 2 else 1 - chip, core]
        peer = chip_peer if kind == 0 else core_peer
        return remote(place, place, c_send.at[kind], c_recv.at[kind], peer)

    def span_copy(d):
        place = cache_all.at[z]
        return remote(place, place, c_send.at[2 + d], c_recv.at[2 + d], peers[d - 1])

    cache_all[z, chip, core] = rows_ref[...]

    expert_id = lax.broadcasted_iota(jnp.int32, (EXPERTS, count), 0)
    member = jnp.zeros((EXPERTS, count), jnp.float32)
    weight = jnp.zeros((EXPERTS, count), jnp.float32)
    for k in range(routes_ref.shape[0]):
        hit = routes_ref[k : k + 1, :] == expert_id
        member = member + jnp.where(hit, 1.0, 0.0)
        weight = weight + jnp.where(hit, rw_ref[k : k + 1, :], 0.0)
    before = jnp.where(
        lax.broadcasted_iota(jnp.int32, (count, count), 0)
        < lax.broadcasted_iota(jnp.int32, (count, count), 1),
        1.0,
        0.0,
    ).astype(jnp.bfloat16)
    rank = jnp.dot(member.astype(jnp.bfloat16), before, preferred_element_type=jnp.float32)
    info_mine[0:EXPERTS, 0:count] = jnp.where(member > 0.5, rank, -1000.0)
    info_mine[EXPERTS : 2 * EXPERTS, 0:count] = weight
    info_mine[:, count:] = jnp.zeros((2 * EXPERTS, info_mine.shape[1] - count), jnp.float32)

    for d in range(1, sources):
        info_copy(d).start()
    for d in range(1, sources):
        token_copy(d).start()
    block_copy(0).start()
    block_copy(1).start()
    tok_all[0:count, :] = tok_ref[...]
    for d in range(1, sources):
        info_copy(d).wait_recv()
    rows = [info_mine[:, 0:count]] + [info_all[d, :, 0:count] for d in range(1, sources)]
    rows = [r + jnp.where(
        lax.broadcasted_iota(jnp.int32, r.shape, 0) < EXPERTS, float(d * MOST), 0.0
    ) for d, r in enumerate(rows)]
    info_row[...] = jnp.concatenate(rows, axis=1)
    for d in range(1, sources):
        token_copy(d).wait_recv()

    slot_id = lax.broadcasted_iota(jnp.int32, (slots, sources * count), 0).astype(jnp.float32)

    def placing(e):
        row = info_row[pl.ds(z * experts + e, 1), :]
        return row == slot_id

    def core_copy(e):
        return remote(send1.at[e], recv1.at[e], s1_send.at[e], s1_recv.at[e], core_peer)

    def chip_copy(e):
        return remote(send2.at[e], recv2.at[e], s2_send.at[e], s2_recv.at[e], chip_peer)

    mine = core * 2 + chip
    theirs = core * 2 + (1 - chip)

    def hid_copy(e, kind):
        q = mine if kind < 2 else theirs
        peer = chip_peer if kind == 0 else core_peer
        return remote(hid.at[e, q], hid.at[e, q], h_send.at[e, kind], h_recv.at[e, kind], peer)

    def project(e):
        weight_copy(wg_ref, 0, e).wait()
        weight_copy(wu_ref, 1, e).wait()
        one_hot = jnp.where(placing(e), 1.0, 0.0).astype(jnp.bfloat16)
        xbuf[...] = jnp.dot(
            one_hot, tok_all[...], preferred_element_type=jnp.float32
        ).astype(jnp.bfloat16)
        gate_slot = lax.rem(2 * e, GATE_SLOTS)
        for where_to, part in ((send1, 1 - core), (own, core)):
            cols = pl.ds(pl.multiple_of(part * half, half), half)
            for which in range(2):
                where_to[e, :, which * half : (which + 1) * half] = jnp.dot(
                    xbuf[...],
                    wslots[gate_slot + which, :, cols],
                    preferred_element_type=jnp.float32,
                )
            if where_to is send1:
                core_copy(e).start()

        @pl.when(e + GATE_SLOTS // 2 < experts)
        def _():
            weight_copy(wg_ref, 0, e + GATE_SLOTS // 2).start()
            weight_copy(wu_ref, 1, e + GATE_SLOTS // 2).start()

    def add_core(e):
        core_copy(e).wait_recv()
        for which in range(2):
            keep = pl.ds(pl.multiple_of(which * half + chip * quarter, quarter), quarter)
            give = pl.ds(pl.multiple_of(which * half + (1 - chip) * quarter, quarter), quarter)
            send2[e, :, which * quarter : (which + 1) * quarter] = (
                own[e, :, give] + recv1[e, :, give]
            ).astype(jnp.bfloat16)
        chip_copy(e).start()
        for which in range(2):
            keep = pl.ds(pl.multiple_of(which * half + chip * quarter, quarter), quarter)
            own[e, :, keep] = own[e, :, keep] + recv1[e, :, keep]

    def activate(e):
        chip_copy(e).wait_recv()
        sums = []
        for which in range(2):
            keep = pl.ds(pl.multiple_of(which * half + chip * quarter, quarter), quarter)
            got = recv2[e, :, which * quarter : (which + 1) * quarter]
            sums.append(own[e, :, keep] + got.astype(jnp.float32))
        w_row = info_row[pl.ds(EXPERTS + z * experts + e, 1), :]
        w_slot = jnp.sum(jnp.where(placing(e), w_row, 0.0), axis=1, keepdims=True)
        hid[e, mine] = (jax.nn.silu(sums[0]) * sums[1] * w_slot).astype(jnp.bfloat16)
        hid_copy(e, 0).start()
        hid_copy(e, 1).start()

    def forward(e):
        hid_copy(e, 0).wait_recv()
        hid_copy(e, 2).start()

    def finish(e):
        hid_copy(e, 1).wait_recv()
        hid_copy(e, 2).wait_recv()
        one_hot = jnp.where(placing(e), 1.0, 0.0).astype(jnp.bfloat16)
        for q in range(4):
            hs[:, q * quarter : (q + 1) * quarter] = lax.dot_general(
                one_hot,
                hid[e, q],
                (((0,), (0,)), ((), ())),
                preferred_element_type=jnp.float32,
            ).astype(jnp.bfloat16)
        down_copy(e).wait()
        slot = lax.rem(e, DOWN_SLOTS)

        for j in range(0, width, 256):
            acc[:, j : j + 256] += jnp.dot(
                hs[...], dslots[slot, :, j : j + 256], preferred_element_type=jnp.float32
            )

        @pl.when(e + DOWN_SLOTS < experts)
        def _():
            down_copy(e + DOWN_SLOTS).start()

    acc[...] = jnp.zeros_like(acc)

    def step(i, carry):
        for lag, stage in enumerate((project, add_core, activate, forward, finish)):

            @pl.when((i >= lag) & (i - lag < experts))
            def _():
                stage(i - lag)

        @pl.when(i == 1)
        def _():
            block_copy(0).wait_recv()
            block_copy(2).start()

        @pl.when(i == 3)
        def _():
            block_copy(1).wait_recv()
            block_copy(2).wait_recv()
            for d in range(1, sources):
                span_copy(d).start()

        return carry

    lax.fori_loop(0, experts + 4, step, 0)

    def back_copy(d):
        return remote(
            psend.at[d], precv.at[d], p_send.at[d], p_recv.at[d], {"expert": lax.rem(z + sources - d, sources)}
        )

    for d in range(1, sources):
        psend[d] = acc[d * count : (d + 1) * count, :].astype(jnp.bfloat16)
        back_copy(d).start()
    for d in range(1, sources):
        span_copy(d).wait_recv()
    block = source_ref[0]
    decode_ref[...] = cache_all[
        lax.div(block, 4), lax.rem(lax.div(block, 2), 2), lax.rem(block, 2)
    ]
    total = acc[0:count, :]
    for d in range(1, sources):
        back_copy(d).wait_recv()
        total = total + precv[d].astype(jnp.float32)
    out_ref[...] = total.astype(out_ref.dtype)

    for d in range(1, sources):
        info_copy(d).wait_send()
        token_copy(d).wait_send()
        back_copy(d).wait_send()
        span_copy(d).wait_send()
    for kind in range(3):
        block_copy(kind).wait_send()

    def drain(e, carry):
        core_copy(e).wait_send()
        chip_copy(e).wait_send()
        for kind in range(3):
            hid_copy(e, kind).wait_send()
        return carry

    lax.fori_loop(0, experts, drain, 0)


def fused_kernel(tokens, routes, route_weights, w_gate, w_up, w_down, rows, slot_source):
    sources = lax.axis_size("expert")
    count, width = tokens.shape
    experts, _, ff = w_gate.shape
    slots = sources * MOST
    half, quarter = ff // 2, ff // 4
    bf16, f32 = jnp.bfloat16, jnp.float32
    vmem = pl.BlockSpec(memory_space=pltpu.VMEM)
    hbm = pl.BlockSpec(memory_space=pl.ANY)
    dma = pltpu.SemaphoreType.DMA
    return pl.pallas_call(
        functools.partial(moe_kernel, sources),
        out_shape=(
            jax.ShapeDtypeStruct((count, width), bf16),
            jax.ShapeDtypeStruct(rows.shape, bf16),
        ),
        in_specs=[vmem, vmem, vmem, hbm, hbm, hbm, vmem, pl.BlockSpec(memory_space=pltpu.SMEM)],
        out_specs=(vmem, vmem),
        scratch_shapes=[
            pltpu.VMEM((sources * count, width), bf16),
            pltpu.VMEM((sources, 2 * EXPERTS, 128), f32),
            pltpu.VMEM((2 * EXPERTS, 128), f32),
            pltpu.VMEM((2 * EXPERTS, sources * count), f32),
            pltpu.VMEM((GATE_SLOTS, width, ff), bf16),
            pltpu.VMEM((DOWN_SLOTS, ff, width), bf16),
            pltpu.VMEM((slots, width), bf16),
            pltpu.VMEM((experts, slots, ff), f32),
            pltpu.VMEM((experts, slots, ff), f32),
            pltpu.VMEM((experts, slots, ff), f32),
            pltpu.VMEM((experts, slots, half), bf16),
            pltpu.VMEM((experts, slots, half), bf16),
            pltpu.VMEM((experts, 4, slots, quarter), bf16),
            pltpu.VMEM((sources * count, ff), bf16),
            pltpu.VMEM((sources * count, width), f32),
            pltpu.VMEM((sources, count, width), bf16),
            pltpu.VMEM((sources, count, width), bf16),
            dma((GATE_SLOTS,)),
            dma((DOWN_SLOTS,)),
            dma((sources,)),
            dma((sources,)),
            dma((sources,)),
            dma((sources,)),
            dma((experts,)),
            dma((experts,)),
            dma((experts,)),
            dma((experts,)),
            dma((experts, 3)),
            dma((experts, 3)),
            dma((sources,)),
            dma((sources,)),
            pltpu.VMEM((sources, 2, 2) + rows.shape, bf16),
            dma((2 + sources,)),
            dma((2 + sources,)),
        ],
        compiler_params=pltpu.CompilerParams(
            collective_id=0, has_side_effects=True, vmem_limit_bytes=VMEM_LIMIT
        ),
        cost_estimate=pl.CostEstimate(
            flops=8 * experts * slots * width * ff,
            bytes_accessed=6 * experts * width * ff,
            transcendentals=0,
        ),
    )(tokens, routes.T, route_weights.T, w_gate, w_up, w_down, rows, slot_source)


def experts_plain(tokens, routes, route_weights, w_gate, w_up, w_down):
    experts_here = w_gate.shape[0]
    token_count = routes.shape[0]
    route_count = routes.shape[1]
    feat_width = tokens.shape[1]
    expert_devices = lax.axis_size("expert")
    flat_routes = routes.reshape(-1)
    onehot = (flat_routes[:, None] == jnp.arange(EXPERTS, dtype=jnp.int32)[None, :]).astype(
        jnp.int32
    )
    earlier = jnp.cumsum(onehot, axis=0) - onehot
    dest_row = flat_routes * MOST + jnp.sum(earlier * onehot, axis=1)
    pair_tok = jnp.arange(token_count * route_count, dtype=jnp.int32) // route_count
    slot_table = jnp.full((EXPERTS * MOST,), token_count, jnp.int32).at[dest_row].set(pair_tok)
    padded = jnp.concatenate([tokens, jnp.zeros((1, feat_width), tokens.dtype)], axis=0)
    outgoing = padded[slot_table]
    incoming = lax.all_to_all(outgoing, "expert", split_axis=0, concat_axis=0, tiled=True)
    grouped = incoming.reshape(expert_devices, experts_here, MOST, feat_width)
    gate_part = jnp.einsum("secd,edf->secf", grouped, w_gate, preferred_element_type=jnp.float32)
    up_part = jnp.einsum("secd,edf->secf", grouped, w_up, preferred_element_type=jnp.float32)
    gate_act, up_act = lax.psum((gate_part, up_part), "role")
    hidden = (jax.nn.silu(gate_act) * up_act).astype(jnp.bfloat16)
    result = jnp.einsum(
        "secf,efd->secd", hidden, w_down, preferred_element_type=jnp.float32
    ).astype(jnp.bfloat16)
    returned = lax.all_to_all(
        result.reshape(expert_devices * experts_here * MOST, feat_width),
        "expert",
        split_axis=0,
        concat_axis=0,
        tiled=True,
    )
    picked = returned[dest_row].reshape(token_count, route_count, feat_width)
    mixed_out = jnp.sum(picked * route_weights[:, :, None], axis=1).astype(jnp.bfloat16)
    return mixed_out


def span_rows(latent, norm_gain, prompt_lengths, span_offsets):
    latent_count = latent.shape[0]
    token_index = lax.axis_index(("expert", "role")) * latent_count + jnp.arange(
        latent_count, dtype=jnp.int32
    )
    positions_f = token_positions(token_index, prompt_lengths, span_offsets)
    return latent_rows(latent, norm_gain, positions_f)


def decode_plain(cache_rows, slot_source):
    blocks = cache_rows.reshape(-1, BLK * cache_rows.shape[1])
    shard_piece = lax.all_gather(blocks, ("expert", "role"), axis=0, tiled=True)
    block_ids = jnp.arange(shard_piece.shape[0], dtype=jnp.int32)
    picker = (slot_source[:, None] == block_ids[None, :]).astype(jnp.bfloat16)
    decode_cache = jnp.dot(picker, shard_piece, preferred_element_type=jnp.float32).astype(
        jnp.bfloat16
    )
    return decode_cache


def local(
    tokens,
    routes,
    route_weights,
    w_gate,
    w_up,
    w_down,
    latent,
    norm_gain,
    prompt_lengths,
    span_offsets,
    slot_source,
):
    rows = span_rows(latent, norm_gain, prompt_lengths, span_offsets)
    if fits_kernel(w_gate, latent):
        mixed_out, block = fused_kernel(
            tokens, routes, route_weights, w_gate, w_up, w_down, rows, slot_source
        )
        decode_cache = block.reshape(1, -1)
    else:
        mixed_out = experts_plain(tokens, routes, route_weights, w_gate, w_up, w_down)
        decode_cache = decode_plain(rows, slot_source)
    return (mixed_out, decode_cache)


def solution(mesh):
    in_specs = (
        P(("groups", "expert"), "role"),
        P(("groups", "expert"), None),
        P(("groups", "expert"), None),
        P("expert", "role", None),
        P("expert", "role", None),
        P("expert", None, "role"),
        P(("groups", "expert", "role"), None),
        P(),
        P("groups"),
        P("groups"),
        P(("groups", "expert", "role")),
    )
    out_specs = (P(("groups", "expert"), "role"), P(("groups", "expert", "role"), None))
    return jax.shard_map(local, mesh=mesh, in_specs=in_specs, out_specs=out_specs, check_vma=False)
```

```python
import functools
import math

import jax
import jax.numpy as jnp
import numpy as np
from jax import lax
from jax.experimental import pallas as pl
from jax.experimental.pallas import tpu as pltpu
from jax.sharding import PartitionSpec as P

LAT = 512
ROPE = 64
EXPERTS = 32
BLK = 16
MOST = 32


def token_positions(token_index, prompt_lengths, span_offsets):
    starts = jnp.cumsum(prompt_lengths) - prompt_lengths
    inside = (token_index[:, None] >= starts[None, :]) & (
        token_index[:, None] < (starts + prompt_lengths)[None, :]
    )
    placed = span_offsets[None, :] + token_index[:, None] - starts[None, :]
    return jnp.sum(jnp.where(inside, placed, 0), axis=1).astype(jnp.float32)


def latent_rows(latent, norm_gain, positions_f):
    latent_f = latent.astype(jnp.float32)
    compressed = latent_f[:, :LAT]
    rope_part = latent_f[:, LAT:]
    normed = (
        compressed
        * lax.rsqrt(jnp.mean(compressed * compressed, axis=1, keepdims=True) + 1e-06)
        * norm_gain[None, :]
    )
    half_rope = ROPE // 2
    inverse_freq = jnp.exp(
        jnp.arange(half_rope, dtype=jnp.float32) * (-2.0 * math.log(10000.0) / ROPE)
    )
    angles = positions_f[:, None] * inverse_freq[None, :]
    cosine = jnp.cos(angles)
    sine_part = jnp.sin(angles)
    first_half = rope_part[:, :half_rope]
    second_half = rope_part[:, half_rope:]
    rotated = jnp.concatenate(
        [
            first_half * cosine - second_half * sine_part,
            second_half * cosine + first_half * sine_part,
        ],
        axis=1,
    )
    return jnp.concatenate([normed, rotated], axis=1).astype(jnp.bfloat16)


GATE_SLOTS = 4
DOWN_SLOTS = 5
VMEM_LIMIT = 62 * 1024 * 1024


def fits_kernel(tokens, w_gate, latent):
    return (
        lax.axis_size("role") == 4
        and lax.axis_size("expert") * MOST <= 128
        and w_gate.shape[0] >= DOWN_SLOTS
        and latent.shape[0] == BLK
        and 2 * tokens.shape[0] == 128
    )


def moe_kernel(
    sources,
    tok_ref,
    info_ref,
    wg_ref,
    wu_ref,
    wd_ref,
    latent_ref,
    gain_ref,
    freq_ref,
    lengths_ref,
    offsets_ref,
    source_ref,
    out_ref,
    decode_ref,
    tok_all,
    info_all,
    info_row,
    wslots,
    dslots,
    xbuf,
    own,
    send1,
    recv1,
    send2,
    recv2,
    hid,
    hs,
    acc,
    psend,
    precv,
    wsem,
    dsem,
    tok_send,
    tok_recv,
    info_send,
    info_recv,
    s1_send,
    s1_recv,
    s2_send,
    s2_recv,
    h_send,
    h_recv,
    p_send,
    p_recv,
    cache_all,
    c_send,
    c_recv,
):
    z = lax.axis_index("expert")
    role = lax.axis_index("role")
    chip = lax.div(role, 2)
    core = lax.rem(role, 2)
    core_peer = {"role": chip * 2 + (1 - core)}
    chip_peer = {"role": (1 - chip) * 2 + core}
    experts = wg_ref.shape[0]
    count = tok_ref.shape[0]
    width = tok_ref.shape[1]
    ff = wg_ref.shape[2]
    half = ff // 2
    quarter = ff // 4
    slots = sources * MOST
    peers = [{"expert": lax.rem(z + d, sources)} for d in range(1, sources)]

    def weight_copy(ref, which, e):
        slot = lax.rem(2 * e + which, GATE_SLOTS)
        return pltpu.make_async_copy(ref.at[e], wslots.at[slot], wsem.at[slot])

    def down_copy(e):
        slot = lax.rem(e, DOWN_SLOTS)
        return pltpu.make_async_copy(wd_ref.at[e], dslots.at[slot], dsem.at[slot])

    for e in range(GATE_SLOTS // 2):
        weight_copy(wg_ref, 0, e).start()
        weight_copy(wu_ref, 1, e).start()
    for e in range(DOWN_SLOTS):
        down_copy(e).start()

    barrier = pltpu.get_barrier_semaphore()
    everyone = peers + [core_peer, chip_peer]
    for peer in everyone:
        pl.semaphore_signal(barrier, inc=1, device_id=peer, device_id_type=pl.DeviceIdType.MESH)
    pl.semaphore_wait(barrier, len(everyone))

    def remote(src, dst, send_sem, recv_sem, peer):
        return pltpu.make_async_remote_copy(
            src_ref=src,
            dst_ref=dst,
            send_sem=send_sem,
            recv_sem=recv_sem,
            device_id=peer,
            device_id_type=pl.DeviceIdType.MESH,
        )

    onward = ({"expert": lax.min(z + 1, sources - 1)}, {"expert": lax.max(z - 1, 0)})

    def sends(way, k):
        return (z - k >= 0) & (z < sources - 1) if way == 0 else (z + k < sources) & (z > 0)

    def gets(way, k):
        return z - 1 - k >= 0 if way == 0 else z + 1 + k < sources

    def at_end(way):
        return z == sources - 1 if way == 0 else z == 0

    def token_hop(way, k, arriving=False):
        back = k + 1 if arriving else k
        block = jnp.clip(z - back if way == 0 else z + back, 0, sources - 1)
        place = tok_all.at[pl.ds(pl.multiple_of(block * count, count), count)]
        src = tok_ref if k == 0 and not arriving else place
        return remote(src, place, tok_send.at[way, k], tok_recv.at[way, k], onward[way])

    def info_copy(d, arriving=False):
        place = info_all.at[lax.rem(z + sources - d, sources) if arriving else z]
        return remote(
            place if arriving else info_ref, place, info_send.at[d], info_recv.at[d], peers[d - 1]
        )

    def block_copy(kind):
        place = cache_all.at[z, chip if kind < 2 else 1 - chip, core]
        peer = chip_peer if kind == 0 else core_peer
        return remote(place, place, c_send.at[kind], c_recv.at[kind], peer)

    def span_copy(d):
        place = cache_all.at[z]
        return remote(place, place, c_send.at[2 + d], c_recv.at[2 + d], peers[d - 1])

    for d in range(1, sources):
        info_copy(d).start()
    for way in range(2):

        @pl.when(sends(way, 0))
        def _():
            token_hop(way, 0).start()

    tok_all[pl.ds(pl.multiple_of(z * count, count), count), :] = tok_ref[...]
    info_all[z] = info_ref[...]
    acc[...] = jnp.zeros_like(acc)

    span_rows_here = latent_ref.shape[0]
    at = (z * 4 + role) * span_rows_here + lax.broadcasted_iota(jnp.int32, (span_rows_here, 1), 0)
    position = jnp.zeros((span_rows_here, 1), jnp.int32)
    start = jnp.int32(0)
    for p in range(lengths_ref.shape[0]):
        stop = start + lengths_ref[p]
        position += jnp.where((at >= start) & (at < stop), offsets_ref[p] + at - start, 0)
        start = stop
    angle = position.astype(jnp.float32) * freq_ref[...]
    turns = jnp.floor(angle * (0.5 / math.pi) + 0.5)
    angle = (angle - turns * 6.28125) - turns * (2.0 * math.pi - 6.28125)
    cosine, sine = jnp.cos(angle), jnp.sin(angle)
    latent_f = latent_ref[...].astype(jnp.float32)
    compressed = latent_f[:, :LAT]
    mean_square = jnp.mean(compressed * compressed, axis=1, keepdims=True)
    normed = compressed * lax.rsqrt(mean_square + 1e-06) * gain_ref[...]
    first = latent_f[:, LAT : LAT + ROPE // 2]
    second = latent_f[:, LAT + ROPE // 2 :]
    rotated = jnp.concatenate(
        [first * cosine - second * sine, second * cosine + first * sine], axis=1
    )
    cache_all[z, chip, core, :, :LAT] = normed.astype(jnp.bfloat16)
    cache_all[z, chip, core, :, LAT:] = rotated.astype(jnp.bfloat16)
    block_copy(0).start()
    block_copy(1).start()

    for d in range(1, sources):
        info_copy(d, True).wait_recv()
    named = jnp.concatenate([info_all[s, :, :count] for s in range(sources)], axis=1)
    weights = jnp.concatenate([info_all[s, :, count : 2 * count] for s in range(sources)], axis=1)
    total_tokens = sources * count
    expert_id = lax.broadcasted_iota(jnp.int32, (EXPERTS, total_tokens), 0).astype(jnp.float32)
    member = jnp.zeros((EXPERTS, total_tokens), jnp.float32)
    weight = jnp.zeros((EXPERTS, total_tokens), jnp.float32)
    for k in range(info_ref.shape[0]):
        hit = named[k : k + 1, :] == expert_id
        member = member + jnp.where(hit, 1.0, 0.0)
        weight = weight + jnp.where(hit, weights[k : k + 1, :], 0.0)
    earlier = lax.broadcasted_iota(jnp.int32, (total_tokens, total_tokens), 0)
    later = lax.broadcasted_iota(jnp.int32, (total_tokens, total_tokens), 1)
    before = (earlier < later) & (lax.div(earlier, count) == lax.div(later, count))
    rank = jnp.dot(
        member.astype(jnp.bfloat16),
        jnp.where(before, 1.0, 0.0).astype(jnp.bfloat16),
        preferred_element_type=jnp.float32,
    )
    source = lax.div(lax.broadcasted_iota(jnp.int32, (EXPERTS, total_tokens), 1), count)
    first_slot = (source * MOST).astype(jnp.float32)
    info_row[0:EXPERTS, :] = jnp.where(member > 0.5, rank + first_slot, -1.0)
    info_row[EXPERTS : 2 * EXPERTS, :] = weight

    for k in range(1, sources - 1):
        for way in range(2):

            @pl.when(sends(way, k))
            def _():
                token_hop(way, k - 1, True).wait_recv()
                token_hop(way, k).start()

    for k in range(sources - 1):
        for way in range(2):

            @pl.when(gets(way, k) & at_end(way))
            def _():
                token_hop(way, k, True).wait_recv()

    slot_id = lax.broadcasted_iota(jnp.int32, (slots, sources * count), 0).astype(jnp.float32)

    def placing(e):
        row = info_row[pl.ds(z * experts + e, 1), :]
        return row == slot_id

    def core_copy(e):
        return remote(send1.at[e], recv1.at[e], s1_send.at[e], s1_recv.at[e], core_peer)

    def chip_copy(e):
        return remote(send2.at[e], recv2.at[e], s2_send.at[e], s2_recv.at[e], chip_peer)

    mine = core * 2 + chip
    theirs = core * 2 + (1 - chip)

    def hid_copy(e, kind):
        q = mine if kind < 2 else theirs
        peer = chip_peer if kind == 0 else core_peer
        return remote(hid.at[e, q], hid.at[e, q], h_send.at[e, kind], h_recv.at[e, kind], peer)

    def project(e):
        weight_copy(wg_ref, 0, e).wait()
        weight_copy(wu_ref, 1, e).wait()
        one_hot = jnp.where(placing(e), 1.0, 0.0).astype(jnp.bfloat16)
        xbuf[...] = jnp.dot(
            one_hot, tok_all[...], preferred_element_type=jnp.float32
        ).astype(jnp.bfloat16)
        gate_slot = lax.rem(2 * e, GATE_SLOTS)
        for where_to, part in ((send1, 1 - core), (own, core)):
            cols = pl.ds(pl.multiple_of(part * half, half), half)
            for which in range(2):
                where_to[e, :, which * half : (which + 1) * half] = jnp.dot(
                    xbuf[...],
                    wslots[gate_slot + which, :, cols],
                    preferred_element_type=jnp.float32,
                )
            if where_to is send1:
                core_copy(e).start()

        @pl.when(e + GATE_SLOTS // 2 < experts)
        def _():
            weight_copy(wg_ref, 0, e + GATE_SLOTS // 2).start()
            weight_copy(wu_ref, 1, e + GATE_SLOTS // 2).start()

    def add_core(e):
        core_copy(e).wait_recv()
        for which in range(2):
            keep = pl.ds(pl.multiple_of(which * half + chip * quarter, quarter), quarter)
            give = pl.ds(pl.multiple_of(which * half + (1 - chip) * quarter, quarter), quarter)
            send2[e, :, which * quarter : (which + 1) * quarter] = (
                own[e, :, give] + recv1[e, :, give]
            ).astype(jnp.bfloat16)
        chip_copy(e).start()
        for which in range(2):
            keep = pl.ds(pl.multiple_of(which * half + chip * quarter, quarter), quarter)
            own[e, :, keep] = own[e, :, keep] + recv1[e, :, keep]

    def activate(e):
        chip_copy(e).wait_recv()
        sums = []
        for which in range(2):
            keep = pl.ds(pl.multiple_of(which * half + chip * quarter, quarter), quarter)
            got = recv2[e, :, which * quarter : (which + 1) * quarter]
            sums.append(own[e, :, keep] + got.astype(jnp.float32))
        w_row = info_row[pl.ds(EXPERTS + z * experts + e, 1), :]
        w_slot = jnp.sum(jnp.where(placing(e), w_row, 0.0), axis=1, keepdims=True)
        hid[e, mine] = (jax.nn.silu(sums[0]) * sums[1] * w_slot).astype(jnp.bfloat16)
        hid_copy(e, 0).start()
        hid_copy(e, 1).start()

    def forward(e):
        hid_copy(e, 0).wait_recv()
        hid_copy(e, 2).start()

    def finish(e):
        hid_copy(e, 1).wait_recv()
        hid_copy(e, 2).wait_recv()
        one_hot = jnp.where(placing(e), 1.0, 0.0).astype(jnp.bfloat16)
        for q in range(4):
            hs[:, q * quarter : (q + 1) * quarter] = lax.dot_general(
                one_hot,
                hid[e, q],
                (((0,), (0,)), ((), ())),
                preferred_element_type=jnp.float32,
            ).astype(jnp.bfloat16)
        down_copy(e).wait()
        slot = lax.rem(e, DOWN_SLOTS)

        for j in range(0, width, 256):
            acc[:, j : j + 256] += jnp.dot(
                hs[...], dslots[slot, :, j : j + 256], preferred_element_type=jnp.float32
            )

        @pl.when(e + DOWN_SLOTS < experts)
        def _():
            down_copy(e + DOWN_SLOTS).start()

    def step(i, carry):
        for lag, stage in enumerate((project, add_core, activate, forward, finish)):

            @pl.when((i >= lag) & (i - lag < experts))
            def _():
                stage(i - lag)

        @pl.when(i == 1)
        def _():
            block_copy(0).wait_recv()
            block_copy(2).start()

        @pl.when(i == 3)
        def _():
            block_copy(1).wait_recv()
            block_copy(2).wait_recv()
            for d in range(1, sources):
                span_copy(d).start()

        return carry

    lax.fori_loop(0, experts + 4, step, 0)

    def back_hop(way, b):
        return remote(
            psend.at[way, b], precv.at[way, b], p_send.at[way, b], p_recv.at[way, b], onward[way]
        )

    def passes(way, b):
        return z < b if way == 0 else z > b

    def hand_on(way, b):
        @pl.when(passes(way, b))
        def _():
            rows = slice(b * count, (b + 1) * count)

            @pl.when(gets(way, 0))
            def _():
                back_hop(way, b).wait_recv()
                psend[way, b] = (acc[rows, :] + precv[way, b].astype(jnp.float32)).astype(
                    jnp.bfloat16
                )

            @pl.when(jnp.logical_not(gets(way, 0)))
            def _():
                psend[way, b] = acc[rows, :].astype(jnp.bfloat16)

            back_hop(way, b).start()

    for step_back in range(sources - 1):
        hand_on(0, sources - 1 - step_back)
        hand_on(1, step_back)

    for d in range(1, sources):
        span_copy(d).wait_recv()
    block = source_ref[0]
    decode_ref[...] = cache_all[
        lax.div(block, 4), lax.rem(lax.div(block, 2), 2), lax.rem(block, 2)
    ]
    mine_rows = pl.ds(pl.multiple_of(z * count, count), count)
    for way in range(2):

        @pl.when(gets(way, 0))
        def _():
            back_hop(way, z).wait_recv()
            acc[mine_rows, :] += precv[way, z].astype(jnp.float32)

    out_ref[...] = acc[mine_rows, :].astype(out_ref.dtype)

    for d in range(1, sources):
        info_copy(d).wait_send()
        span_copy(d).wait_send()
    for way in range(2):
        for k in range(sources - 1):

            @pl.when(sends(way, k))
            def _():
                token_hop(way, k).wait_send()

        for b in range(sources):

            @pl.when(passes(way, b))
            def _():
                back_hop(way, b).wait_send()

    for kind in range(3):
        block_copy(kind).wait_send()

    def drain(e, carry):
        core_copy(e).wait_send()
        chip_copy(e).wait_send()
        for kind in range(3):
            hid_copy(e, kind).wait_send()
        return carry

    lax.fori_loop(0, experts, drain, 0)


def fused_kernel(
    tokens,
    routes,
    route_weights,
    w_gate,
    w_up,
    w_down,
    latent,
    norm_gain,
    prompt_lengths,
    span_offsets,
    slot_source,
):
    sources = lax.axis_size("expert")
    count, width = tokens.shape
    experts, _, ff = w_gate.shape
    slots = sources * MOST
    half, quarter = ff // 2, ff // 4
    bf16, f32 = jnp.bfloat16, jnp.float32
    info = jnp.concatenate([routes.T.astype(f32), route_weights.T], axis=1)
    half_rope = ROPE // 2
    freq = 10000.0 ** (-2.0 * np.arange(half_rope) / ROPE)
    vmem = pl.BlockSpec(memory_space=pltpu.VMEM)
    smem = pl.BlockSpec(memory_space=pltpu.SMEM)
    hbm = pl.BlockSpec(memory_space=pl.ANY)
    dma = pltpu.SemaphoreType.DMA
    return pl.pallas_call(
        functools.partial(moe_kernel, sources),
        out_shape=(
            jax.ShapeDtypeStruct((count, width), bf16),
            jax.ShapeDtypeStruct(latent.shape, bf16),
        ),
        in_specs=[vmem, vmem, hbm, hbm, hbm, vmem, vmem, vmem, smem, smem, smem],
        out_specs=(vmem, vmem),
        scratch_shapes=[
            pltpu.VMEM((sources * count, width), bf16),
            pltpu.VMEM((sources,) + info.shape, f32),
            pltpu.VMEM((2 * EXPERTS, sources * count), f32),
            pltpu.VMEM((GATE_SLOTS, width, ff), bf16),
            pltpu.VMEM((DOWN_SLOTS, ff, width), bf16),
            pltpu.VMEM((slots, width), bf16),
            pltpu.VMEM((experts, slots, ff), f32),
            pltpu.VMEM((experts, slots, ff), f32),
            pltpu.VMEM((experts, slots, ff), f32),
            pltpu.VMEM((experts, slots, half), bf16),
            pltpu.VMEM((experts, slots, half), bf16),
            pltpu.VMEM((experts, 4, slots, quarter), bf16),
            pltpu.VMEM((sources * count, ff), bf16),
            pltpu.VMEM((sources * count, width), f32),
            pltpu.VMEM((2, sources, count, width), bf16),
            pltpu.VMEM((2, sources, count, width), bf16),
            dma((GATE_SLOTS,)),
            dma((DOWN_SLOTS,)),
            dma((2, sources)),
            dma((2, sources)),
            dma((sources,)),
            dma((sources,)),
            dma((experts,)),
            dma((experts,)),
            dma((experts,)),
            dma((experts,)),
            dma((experts, 3)),
            dma((experts, 3)),
            dma((2, sources)),
            dma((2, sources)),
            pltpu.VMEM((sources, 2, 2) + latent.shape, bf16),
            dma((2 + sources,)),
            dma((2 + sources,)),
        ],
        compiler_params=pltpu.CompilerParams(
            collective_id=0, has_side_effects=True, vmem_limit_bytes=VMEM_LIMIT
        ),
        cost_estimate=pl.CostEstimate(
            flops=8 * experts * slots * width * ff,
            bytes_accessed=6 * experts * width * ff,
            transcendentals=0,
        ),
    )(
        tokens,
        info,
        w_gate,
        w_up,
        w_down,
        latent,
        norm_gain[None, :],
        jnp.asarray(freq[None, :], f32),
        prompt_lengths,
        span_offsets,
        slot_source,
    )


def experts_plain(tokens, routes, route_weights, w_gate, w_up, w_down):
    experts_here = w_gate.shape[0]
    token_count = routes.shape[0]
    route_count = routes.shape[1]
    feat_width = tokens.shape[1]
    expert_devices = lax.axis_size("expert")
    flat_routes = routes.reshape(-1)
    onehot = (flat_routes[:, None] == jnp.arange(EXPERTS, dtype=jnp.int32)[None, :]).astype(
        jnp.int32
    )
    earlier = jnp.cumsum(onehot, axis=0) - onehot
    dest_row = flat_routes * MOST + jnp.sum(earlier * onehot, axis=1)
    pair_tok = jnp.arange(token_count * route_count, dtype=jnp.int32) // route_count
    slot_table = jnp.full((EXPERTS * MOST,), token_count, jnp.int32).at[dest_row].set(pair_tok)
    padded = jnp.concatenate([tokens, jnp.zeros((1, feat_width), tokens.dtype)], axis=0)
    outgoing = padded[slot_table]
    incoming = lax.all_to_all(outgoing, "expert", split_axis=0, concat_axis=0, tiled=True)
    grouped = incoming.reshape(expert_devices, experts_here, MOST, feat_width)
    gate_part = jnp.einsum("secd,edf->secf", grouped, w_gate, preferred_element_type=jnp.float32)
    up_part = jnp.einsum("secd,edf->secf", grouped, w_up, preferred_element_type=jnp.float32)
    gate_act, up_act = lax.psum((gate_part, up_part), "role")
    hidden = (jax.nn.silu(gate_act) * up_act).astype(jnp.bfloat16)
    result = jnp.einsum(
        "secf,efd->secd", hidden, w_down, preferred_element_type=jnp.float32
    ).astype(jnp.bfloat16)
    returned = lax.all_to_all(
        result.reshape(expert_devices * experts_here * MOST, feat_width),
        "expert",
        split_axis=0,
        concat_axis=0,
        tiled=True,
    )
    picked = returned[dest_row].reshape(token_count, route_count, feat_width)
    mixed_out = jnp.sum(picked * route_weights[:, :, None], axis=1).astype(jnp.bfloat16)
    return mixed_out


def span_rows(latent, norm_gain, prompt_lengths, span_offsets):
    latent_count = latent.shape[0]
    token_index = lax.axis_index(("expert", "role")) * latent_count + jnp.arange(
        latent_count, dtype=jnp.int32
    )
    positions_f = token_positions(token_index, prompt_lengths, span_offsets)
    return latent_rows(latent, norm_gain, positions_f)


def decode_plain(cache_rows, slot_source):
    blocks = cache_rows.reshape(-1, BLK * cache_rows.shape[1])
    shard_piece = lax.all_gather(blocks, ("expert", "role"), axis=0, tiled=True)
    block_ids = jnp.arange(shard_piece.shape[0], dtype=jnp.int32)
    picker = (slot_source[:, None] == block_ids[None, :]).astype(jnp.bfloat16)
    decode_cache = jnp.dot(picker, shard_piece, preferred_element_type=jnp.float32).astype(
        jnp.bfloat16
    )
    return decode_cache


def local(
    tokens,
    routes,
    route_weights,
    w_gate,
    w_up,
    w_down,
    latent,
    norm_gain,
    prompt_lengths,
    span_offsets,
    slot_source,
):
    if fits_kernel(tokens, w_gate, latent):
        mixed_out, block = fused_kernel(
            tokens,
            routes,
            route_weights,
            w_gate,
            w_up,
            w_down,
            latent,
            norm_gain,
            prompt_lengths,
            span_offsets,
            slot_source,
        )
        decode_cache = block.reshape(1, -1)
    else:
        mixed_out = experts_plain(tokens, routes, route_weights, w_gate, w_up, w_down)
        rows = span_rows(latent, norm_gain, prompt_lengths, span_offsets)
        decode_cache = decode_plain(rows, slot_source)
    return (mixed_out, decode_cache)


def solution(mesh):
    in_specs = (
        P(("groups", "expert"), "role"),
        P(("groups", "expert"), None),
        P(("groups", "expert"), None),
        P("expert", "role", None),
        P("expert", "role", None),
        P("expert", None, "role"),
        P(("groups", "expert", "role"), None),
        P(),
        P("groups"),
        P("groups"),
        P(("groups", "expert", "role")),
    )
    out_specs = (P(("groups", "expert"), "role"), P(("groups", "expert", "role"), None))
    return jax.shard_map(local, mesh=mesh, in_specs=in_specs, out_specs=out_specs, check_vma=False)
```

```python
import functools
import math

import jax
import jax.numpy as jnp
import numpy as np
from jax import lax
from jax.experimental import pallas as pl
from jax.experimental.pallas import tpu as pltpu
from jax.sharding import PartitionSpec as P

LAT = 512
ROPE = 64
EXPERTS = 32
BLK = 16
MOST = 32


def token_positions(token_index, prompt_lengths, span_offsets):
    starts = jnp.cumsum(prompt_lengths) - prompt_lengths
    inside = (token_index[:, None] >= starts[None, :]) & (
        token_index[:, None] < (starts + prompt_lengths)[None, :]
    )
    placed = span_offsets[None, :] + token_index[:, None] - starts[None, :]
    return jnp.sum(jnp.where(inside, placed, 0), axis=1).astype(jnp.float32)


def latent_rows(latent, norm_gain, positions_f):
    latent_f = latent.astype(jnp.float32)
    compressed = latent_f[:, :LAT]
    rope_part = latent_f[:, LAT:]
    normed = (
        compressed
        * lax.rsqrt(jnp.mean(compressed * compressed, axis=1, keepdims=True) + 1e-06)
        * norm_gain[None, :]
    )
    half_rope = ROPE // 2
    inverse_freq = jnp.exp(
        jnp.arange(half_rope, dtype=jnp.float32) * (-2.0 * math.log(10000.0) / ROPE)
    )
    angles = positions_f[:, None] * inverse_freq[None, :]
    cosine = jnp.cos(angles)
    sine_part = jnp.sin(angles)
    first_half = rope_part[:, :half_rope]
    second_half = rope_part[:, half_rope:]
    rotated = jnp.concatenate(
        [
            first_half * cosine - second_half * sine_part,
            second_half * cosine + first_half * sine_part,
        ],
        axis=1,
    )
    return jnp.concatenate([normed, rotated], axis=1).astype(jnp.bfloat16)


GATE_SLOTS = 4
DOWN_SLOTS = 5
VMEM_LIMIT = 62 * 1024 * 1024


def fits_kernel(tokens, w_gate, latent):
    return (
        lax.axis_size("role") == 4
        and lax.axis_size("expert") * MOST <= 128
        and w_gate.shape[0] >= DOWN_SLOTS
        and latent.shape[0] == BLK
        and 2 * tokens.shape[0] == 128
    )


def moe_kernel(
    sources,
    tok_ref,
    info_ref,
    wg_ref,
    wu_ref,
    wd_ref,
    latent_ref,
    gain_ref,
    freq_ref,
    lengths_ref,
    offsets_ref,
    source_ref,
    out_ref,
    decode_ref,
    tok_all,
    info_all,
    info_row,
    wslots,
    dslots,
    xbuf,
    own,
    send1,
    recv1,
    send2,
    recv2,
    hid,
    hs,
    acc,
    psend,
    precv,
    wsem,
    dsem,
    tok_send,
    tok_recv,
    info_send,
    info_recv,
    s1_send,
    s1_recv,
    s2_send,
    s2_recv,
    h_send,
    h_recv,
    p_send,
    p_recv,
    cache_all,
    c_send,
    c_recv,
):
    z = lax.axis_index("expert")
    role = lax.axis_index("role")
    chip = lax.div(role, 2)
    core = lax.rem(role, 2)
    core_peer = {"role": chip * 2 + (1 - core)}
    chip_peer = {"role": (1 - chip) * 2 + core}
    experts = wg_ref.shape[0]
    count = tok_ref.shape[0]
    width = tok_ref.shape[1]
    ff = wg_ref.shape[2]
    half = ff // 2
    quarter = ff // 4
    slots = sources * MOST
    peers = [{"expert": lax.rem(z + d, sources)} for d in range(1, sources)]

    def weight_copy(ref, which, e):
        slot = lax.rem(2 * e + which, GATE_SLOTS)
        return pltpu.make_async_copy(ref.at[e], wslots.at[slot], wsem.at[slot])

    def down_copy(e):
        slot = lax.rem(e, DOWN_SLOTS)
        return pltpu.make_async_copy(wd_ref.at[e], dslots.at[slot], dsem.at[slot])

    for e in range(GATE_SLOTS // 2):
        weight_copy(wg_ref, 0, e).start()
        weight_copy(wu_ref, 1, e).start()
    for e in range(DOWN_SLOTS):
        down_copy(e).start()

    barrier = pltpu.get_barrier_semaphore()
    everyone = peers + [core_peer, chip_peer]
    for peer in everyone:
        pl.semaphore_signal(barrier, inc=1, device_id=peer, device_id_type=pl.DeviceIdType.MESH)
    pl.semaphore_wait(barrier, len(everyone))

    def remote(src, dst, send_sem, recv_sem, peer):
        return pltpu.make_async_remote_copy(
            src_ref=src,
            dst_ref=dst,
            send_sem=send_sem,
            recv_sem=recv_sem,
            device_id=peer,
            device_id_type=pl.DeviceIdType.MESH,
        )

    onward = ({"expert": lax.min(z + 1, sources - 1)}, {"expert": lax.max(z - 1, 0)})

    def sends(way, k):
        return (z - k >= 0) & (z < sources - 1) if way == 0 else (z + k < sources) & (z > 0)

    def gets(way, k):
        return z - 1 - k >= 0 if way == 0 else z + 1 + k < sources

    def at_end(way):
        return z == sources - 1 if way == 0 else z == 0

    def token_hop(way, k, arriving=False):
        back = k + 1 if arriving else k
        block = jnp.clip(z - back if way == 0 else z + back, 0, sources - 1)
        place = tok_all.at[pl.ds(pl.multiple_of(block * count, count), count)]
        src = tok_ref if k == 0 and not arriving else place
        return remote(src, place, tok_send.at[way, k], tok_recv.at[way, k], onward[way])

    def info_copy(d, arriving=False):
        place = info_all.at[lax.rem(z + sources - d, sources) if arriving else z]
        return remote(
            place if arriving else info_ref, place, info_send.at[d], info_recv.at[d], peers[d - 1]
        )

    def block_copy(kind):
        place = cache_all.at[z, chip if kind < 2 else 1 - chip, core]
        peer = chip_peer if kind == 0 else core_peer
        return remote(place, place, c_send.at[kind], c_recv.at[kind], peer)

    def span_copy(d):
        place = cache_all.at[z]
        return remote(place, place, c_send.at[2 + d], c_recv.at[2 + d], peers[d - 1])

    for d in range(1, sources):
        info_copy(d).start()
    for way in range(2):

        @pl.when(sends(way, 0))
        def _():
            token_hop(way, 0).start()

    tok_all[pl.ds(pl.multiple_of(z * count, count), count), :] = tok_ref[...]
    info_all[z] = info_ref[...]
    acc[...] = jnp.zeros_like(acc)

    span_rows_here = latent_ref.shape[0]
    at = (z * 4 + role) * span_rows_here + lax.broadcasted_iota(jnp.int32, (span_rows_here, 1), 0)
    position = jnp.zeros((span_rows_here, 1), jnp.int32)
    start = jnp.int32(0)
    for p in range(lengths_ref.shape[0]):
        stop = start + lengths_ref[p]
        position += jnp.where((at >= start) & (at < stop), offsets_ref[p] + at - start, 0)
        start = stop
    angle = position.astype(jnp.float32) * freq_ref[...]
    turns = jnp.floor(angle * (0.5 / math.pi) + 0.5)
    angle = (angle - turns * 6.28125) - turns * (2.0 * math.pi - 6.28125)
    cosine, sine = jnp.cos(angle), jnp.sin(angle)
    latent_f = latent_ref[...].astype(jnp.float32)
    compressed = latent_f[:, :LAT]
    mean_square = jnp.mean(compressed * compressed, axis=1, keepdims=True)
    normed = compressed * lax.rsqrt(mean_square + 1e-06) * gain_ref[...]
    first = latent_f[:, LAT : LAT + ROPE // 2]
    second = latent_f[:, LAT + ROPE // 2 :]
    rotated = jnp.concatenate(
        [first * cosine - second * sine, second * cosine + first * sine], axis=1
    )
    cache_all[z, chip, core, :, :LAT] = normed.astype(jnp.bfloat16)
    cache_all[z, chip, core, :, LAT:] = rotated.astype(jnp.bfloat16)
    block_copy(0).start()
    block_copy(1).start()

    for d in range(1, sources):
        info_copy(d, True).wait_recv()
    named = jnp.concatenate([info_all[s, :, :count] for s in range(sources)], axis=1)
    weights = jnp.concatenate([info_all[s, :, count : 2 * count] for s in range(sources)], axis=1)
    total_tokens = sources * count
    expert_id = lax.broadcasted_iota(jnp.int32, (EXPERTS, total_tokens), 0).astype(jnp.float32)
    member = jnp.zeros((EXPERTS, total_tokens), jnp.float32)
    weight = jnp.zeros((EXPERTS, total_tokens), jnp.float32)
    for k in range(info_ref.shape[0]):
        hit = named[k : k + 1, :] == expert_id
        member = member + jnp.where(hit, 1.0, 0.0)
        weight = weight + jnp.where(hit, weights[k : k + 1, :], 0.0)
    earlier = lax.broadcasted_iota(jnp.int32, (total_tokens, total_tokens), 0)
    later = lax.broadcasted_iota(jnp.int32, (total_tokens, total_tokens), 1)
    before = (earlier < later) & (lax.div(earlier, count) == lax.div(later, count))
    rank = jnp.dot(
        member.astype(jnp.bfloat16),
        jnp.where(before, 1.0, 0.0).astype(jnp.bfloat16),
        preferred_element_type=jnp.float32,
    )
    source = lax.div(lax.broadcasted_iota(jnp.int32, (EXPERTS, total_tokens), 1), count)
    first_slot = (source * MOST).astype(jnp.float32)
    info_row[0:EXPERTS, :] = jnp.where(member > 0.5, rank + first_slot, -1.0)
    info_row[EXPERTS : 2 * EXPERTS, :] = weight

    for k in range(1, sources - 1):
        for way in range(2):

            @pl.when(sends(way, k))
            def _():
                token_hop(way, k - 1, True).wait_recv()
                token_hop(way, k).start()

    for k in range(sources - 1):
        for way in range(2):

            @pl.when(gets(way, k) & at_end(way))
            def _():
                token_hop(way, k, True).wait_recv()

    slot_id = lax.broadcasted_iota(jnp.int32, (slots, sources * count), 0).astype(jnp.float32)

    def placing(e):
        row = info_row[pl.ds(z * experts + e, 1), :]
        return row == slot_id

    def core_copy(e):
        return remote(send1.at[e], recv1.at[e], s1_send.at[e], s1_recv.at[e], core_peer)

    def chip_copy(e):
        return remote(send2.at[e], recv2.at[e], s2_send.at[e], s2_recv.at[e], chip_peer)

    mine = core * 2 + chip
    theirs = core * 2 + (1 - chip)

    def hid_copy(e, kind):
        q = mine if kind < 2 else theirs
        peer = chip_peer if kind == 0 else core_peer
        return remote(hid.at[e, q], hid.at[e, q], h_send.at[e, kind], h_recv.at[e, kind], peer)

    def project(e):
        weight_copy(wg_ref, 0, e).wait()
        weight_copy(wu_ref, 1, e).wait()
        one_hot = jnp.where(placing(e), 1.0, 0.0).astype(jnp.bfloat16)
        xbuf[...] = jnp.dot(
            one_hot, tok_all[...], preferred_element_type=jnp.float32
        ).astype(jnp.bfloat16)
        gate_slot = lax.rem(2 * e, GATE_SLOTS)
        for where_to, part in ((send1, 1 - core), (own, core)):
            cols = pl.ds(pl.multiple_of(part * half, half), half)
            for which in range(2):
                where_to[e, :, which * half : (which + 1) * half] = jnp.dot(
                    xbuf[...],
                    wslots[gate_slot + which, :, cols],
                    preferred_element_type=jnp.float32,
                )
            if where_to is send1:
                core_copy(e).start()

        @pl.when(e + GATE_SLOTS // 2 < experts)
        def _():
            weight_copy(wg_ref, 0, e + GATE_SLOTS // 2).start()
            weight_copy(wu_ref, 1, e + GATE_SLOTS // 2).start()

    def add_core(e):
        core_copy(e).wait_recv()
        for which in range(2):
            keep = pl.ds(pl.multiple_of(which * half + chip * quarter, quarter), quarter)
            give = pl.ds(pl.multiple_of(which * half + (1 - chip) * quarter, quarter), quarter)
            send2[e, :, which * quarter : (which + 1) * quarter] = (
                own[e, :, give] + recv1[e, :, give]
            ).astype(jnp.bfloat16)
        chip_copy(e).start()
        for which in range(2):
            keep = pl.ds(pl.multiple_of(which * half + chip * quarter, quarter), quarter)
            own[e, :, keep] = own[e, :, keep] + recv1[e, :, keep]

    def activate(e):
        chip_copy(e).wait_recv()
        sums = []
        for which in range(2):
            keep = pl.ds(pl.multiple_of(which * half + chip * quarter, quarter), quarter)
            got = recv2[e, :, which * quarter : (which + 1) * quarter]
            sums.append(own[e, :, keep] + got.astype(jnp.float32))
        w_row = info_row[pl.ds(EXPERTS + z * experts + e, 1), :]
        w_slot = jnp.sum(jnp.where(placing(e), w_row, 0.0), axis=1, keepdims=True)
        hid[e, mine] = (jax.nn.silu(sums[0]) * sums[1] * w_slot).astype(jnp.bfloat16)
        hid_copy(e, 0).start()
        hid_copy(e, 1).start()

    def forward(e):
        hid_copy(e, 0).wait_recv()
        hid_copy(e, 2).start()

    def finish(e):
        hid_copy(e, 1).wait_recv()
        hid_copy(e, 2).wait_recv()
        one_hot = jnp.where(placing(e), 1.0, 0.0).astype(jnp.bfloat16)
        for q in range(4):
            hs[:, q * quarter : (q + 1) * quarter] = lax.dot_general(
                one_hot,
                hid[e, q],
                (((0,), (0,)), ((), ())),
                preferred_element_type=jnp.float32,
            ).astype(jnp.bfloat16)
        down_copy(e).wait()
        slot = lax.rem(e, DOWN_SLOTS)

        for j in range(0, width, 256):
            acc[:, j : j + 256] += jnp.dot(
                hs[...], dslots[slot, :, j : j + 256], preferred_element_type=jnp.float32
            )

        @pl.when(e + DOWN_SLOTS < experts)
        def _():
            down_copy(e + DOWN_SLOTS).start()

    def step(i, carry):
        stages = ((0, project), (1, add_core), (3, activate), (5, forward), (6, finish))
        for lag, stage in stages:

            @pl.when((i >= lag) & (i - lag < experts))
            def _():
                stage(i - lag)

        @pl.when(i == 1)
        def _():
            block_copy(0).wait_recv()
            block_copy(2).start()

        @pl.when(i == 3)
        def _():
            block_copy(1).wait_recv()
            block_copy(2).wait_recv()
            for d in range(1, sources):
                span_copy(d).start()

        return carry

    lax.fori_loop(0, experts + 6, step, 0)

    def back_hop(way, b):
        return remote(
            psend.at[way, b], precv.at[way, b], p_send.at[way, b], p_recv.at[way, b], onward[way]
        )

    def passes(way, b):
        return z < b if way == 0 else z > b

    def hand_on(way, b):
        @pl.when(passes(way, b))
        def _():
            rows = slice(b * count, (b + 1) * count)

            @pl.when(gets(way, 0))
            def _():
                back_hop(way, b).wait_recv()
                psend[way, b] = (acc[rows, :] + precv[way, b].astype(jnp.float32)).astype(
                    jnp.bfloat16
                )

            @pl.when(jnp.logical_not(gets(way, 0)))
            def _():
                psend[way, b] = acc[rows, :].astype(jnp.bfloat16)

            back_hop(way, b).start()

    for step_back in range(sources - 1):
        hand_on(0, sources - 1 - step_back)
        hand_on(1, step_back)

    for d in range(1, sources):
        span_copy(d).wait_recv()
    block = source_ref[0]
    decode_ref[...] = cache_all[
        lax.div(block, 4), lax.rem(lax.div(block, 2), 2), lax.rem(block, 2)
    ]
    mine_rows = pl.ds(pl.multiple_of(z * count, count), count)
    for way in range(2):

        @pl.when(gets(way, 0))
        def _():
            back_hop(way, z).wait_recv()
            acc[mine_rows, :] += precv[way, z].astype(jnp.float32)

    out_ref[...] = acc[mine_rows, :].astype(out_ref.dtype)

    for d in range(1, sources):
        info_copy(d).wait_send()
        span_copy(d).wait_send()
    for way in range(2):
        for k in range(sources - 1):

            @pl.when(sends(way, k))
            def _():
                token_hop(way, k).wait_send()

        for b in range(sources):

            @pl.when(passes(way, b))
            def _():
                back_hop(way, b).wait_send()

    for kind in range(3):
        block_copy(kind).wait_send()

    def drain(e, carry):
        core_copy(e).wait_send()
        chip_copy(e).wait_send()
        for kind in range(3):
            hid_copy(e, kind).wait_send()
        return carry

    lax.fori_loop(0, experts, drain, 0)


def fused_kernel(
    tokens,
    routes,
    route_weights,
    w_gate,
    w_up,
    w_down,
    latent,
    norm_gain,
    prompt_lengths,
    span_offsets,
    slot_source,
):
    sources = lax.axis_size("expert")
    count, width = tokens.shape
    experts, _, ff = w_gate.shape
    slots = sources * MOST
    half, quarter = ff // 2, ff // 4
    bf16, f32 = jnp.bfloat16, jnp.float32
    info = jnp.concatenate([routes.T.astype(f32), route_weights.T], axis=1)
    half_rope = ROPE // 2
    freq = 10000.0 ** (-2.0 * np.arange(half_rope) / ROPE)
    vmem = pl.BlockSpec(memory_space=pltpu.VMEM)
    smem = pl.BlockSpec(memory_space=pltpu.SMEM)
    hbm = pl.BlockSpec(memory_space=pl.ANY)
    dma = pltpu.SemaphoreType.DMA
    return pl.pallas_call(
        functools.partial(moe_kernel, sources),
        out_shape=(
            jax.ShapeDtypeStruct((count, width), bf16),
            jax.ShapeDtypeStruct(latent.shape, bf16),
        ),
        in_specs=[vmem, vmem, hbm, hbm, hbm, vmem, vmem, vmem, smem, smem, smem],
        out_specs=(vmem, vmem),
        scratch_shapes=[
            pltpu.VMEM((sources * count, width), bf16),
            pltpu.VMEM((sources,) + info.shape, f32),
            pltpu.VMEM((2 * EXPERTS, sources * count), f32),
            pltpu.VMEM((GATE_SLOTS, width, ff), bf16),
            pltpu.VMEM((DOWN_SLOTS, ff, width), bf16),
            pltpu.VMEM((slots, width), bf16),
            pltpu.VMEM((experts, slots, ff), f32),
            pltpu.VMEM((experts, slots, ff), f32),
            pltpu.VMEM((experts, slots, ff), f32),
            pltpu.VMEM((experts, slots, half), bf16),
            pltpu.VMEM((experts, slots, half), bf16),
            pltpu.VMEM((experts, 4, slots, quarter), bf16),
            pltpu.VMEM((sources * count, ff), bf16),
            pltpu.VMEM((sources * count, width), f32),
            pltpu.VMEM((2, sources, count, width), bf16),
            pltpu.VMEM((2, sources, count, width), bf16),
            dma((GATE_SLOTS,)),
            dma((DOWN_SLOTS,)),
            dma((2, sources)),
            dma((2, sources)),
            dma((sources,)),
            dma((sources,)),
            dma((experts,)),
            dma((experts,)),
            dma((experts,)),
            dma((experts,)),
            dma((experts, 3)),
            dma((experts, 3)),
            dma((2, sources)),
            dma((2, sources)),
            pltpu.VMEM((sources, 2, 2) + latent.shape, bf16),
            dma((2 + sources,)),
            dma((2 + sources,)),
        ],
        compiler_params=pltpu.CompilerParams(
            collective_id=0, has_side_effects=True, vmem_limit_bytes=VMEM_LIMIT
        ),
        cost_estimate=pl.CostEstimate(
            flops=8 * experts * slots * width * ff,
            bytes_accessed=6 * experts * width * ff,
            transcendentals=0,
        ),
    )(
        tokens,
        info,
        w_gate,
        w_up,
        w_down,
        latent,
        norm_gain[None, :],
        jnp.asarray(freq[None, :], f32),
        prompt_lengths,
        span_offsets,
        slot_source,
    )


def experts_plain(tokens, routes, route_weights, w_gate, w_up, w_down):
    experts_here = w_gate.shape[0]
    token_count = routes.shape[0]
    route_count = routes.shape[1]
    feat_width = tokens.shape[1]
    expert_devices = lax.axis_size("expert")
    flat_routes = routes.reshape(-1)
    onehot = (flat_routes[:, None] == jnp.arange(EXPERTS, dtype=jnp.int32)[None, :]).astype(
        jnp.int32
    )
    earlier = jnp.cumsum(onehot, axis=0) - onehot
    dest_row = flat_routes * MOST + jnp.sum(earlier * onehot, axis=1)
    pair_tok = jnp.arange(token_count * route_count, dtype=jnp.int32) // route_count
    slot_table = jnp.full((EXPERTS * MOST,), token_count, jnp.int32).at[dest_row].set(pair_tok)
    padded = jnp.concatenate([tokens, jnp.zeros((1, feat_width), tokens.dtype)], axis=0)
    outgoing = padded[slot_table]
    incoming = lax.all_to_all(outgoing, "expert", split_axis=0, concat_axis=0, tiled=True)
    grouped = incoming.reshape(expert_devices, experts_here, MOST, feat_width)
    gate_part = jnp.einsum("secd,edf->secf", grouped, w_gate, preferred_element_type=jnp.float32)
    up_part = jnp.einsum("secd,edf->secf", grouped, w_up, preferred_element_type=jnp.float32)
    gate_act, up_act = lax.psum((gate_part, up_part), "role")
    hidden = (jax.nn.silu(gate_act) * up_act).astype(jnp.bfloat16)
    result = jnp.einsum(
        "secf,efd->secd", hidden, w_down, preferred_element_type=jnp.float32
    ).astype(jnp.bfloat16)
    returned = lax.all_to_all(
        result.reshape(expert_devices * experts_here * MOST, feat_width),
        "expert",
        split_axis=0,
        concat_axis=0,
        tiled=True,
    )
    picked = returned[dest_row].reshape(token_count, route_count, feat_width)
    mixed_out = jnp.sum(picked * route_weights[:, :, None], axis=1).astype(jnp.bfloat16)
    return mixed_out


def span_rows(latent, norm_gain, prompt_lengths, span_offsets):
    latent_count = latent.shape[0]
    token_index = lax.axis_index(("expert", "role")) * latent_count + jnp.arange(
        latent_count, dtype=jnp.int32
    )
    positions_f = token_positions(token_index, prompt_lengths, span_offsets)
    return latent_rows(latent, norm_gain, positions_f)


def decode_plain(cache_rows, slot_source):
    blocks = cache_rows.reshape(-1, BLK * cache_rows.shape[1])
    shard_piece = lax.all_gather(blocks, ("expert", "role"), axis=0, tiled=True)
    block_ids = jnp.arange(shard_piece.shape[0], dtype=jnp.int32)
    picker = (slot_source[:, None] == block_ids[None, :]).astype(jnp.bfloat16)
    decode_cache = jnp.dot(picker, shard_piece, preferred_element_type=jnp.float32).astype(
        jnp.bfloat16
    )
    return decode_cache


def local(
    tokens,
    routes,
    route_weights,
    w_gate,
    w_up,
    w_down,
    latent,
    norm_gain,
    prompt_lengths,
    span_offsets,
    slot_source,
):
    if fits_kernel(tokens, w_gate, latent):
        mixed_out, block = fused_kernel(
            tokens,
            routes,
            route_weights,
            w_gate,
            w_up,
            w_down,
            latent,
            norm_gain,
            prompt_lengths,
            span_offsets,
            slot_source,
        )
        decode_cache = block.reshape(1, -1)
    else:
        mixed_out = experts_plain(tokens, routes, route_weights, w_gate, w_up, w_down)
        rows = span_rows(latent, norm_gain, prompt_lengths, span_offsets)
        decode_cache = decode_plain(rows, slot_source)
    return (mixed_out, decode_cache)


def solution(mesh):
    in_specs = (
        P(("groups", "expert"), "role"),
        P(("groups", "expert"), None),
        P(("groups", "expert"), None),
        P("expert", "role", None),
        P("expert", "role", None),
        P("expert", None, "role"),
        P(("groups", "expert", "role"), None),
        P(),
        P("groups"),
        P("groups"),
        P(("groups", "expert", "role")),
    )
    out_specs = (P(("groups", "expert"), "role"), P(("groups", "expert", "role"), None))
    return jax.shard_map(local, mesh=mesh, in_specs=in_specs, out_specs=out_specs, check_vma=False)
```
